128 devices in a mesh: chan: 32 (over z_lo, x, y), seg: 4 (over z_hi, core).
Axes of the slice: x: 4, y: 4, z: 4 (z_hi: 2, z_lo: 2; z = z_hi * 2 + z_lo), core: 2. Of those that a mesh axis runs over, the one named last changes fastest.
Arguments:
- traces: bfloat16 [1024, 16, 8192], P('chan', 'seg'), may hold values from -6 to 6
- alive: int32 [1024], P('chan'), may hold values 0 or 1
- pair_chan: int32 [4096, 2], P('chan'), may hold values from 0 to 1023, as said below
- lag_window: int32 [4096], P(('chan', 'seg')), may hold values from 4 to 256
Outputs:
- correlation: float32 [4096, 512], P(('chan', 'seg'))
The draws below stay inside these ranges and needn't reach their ends.
Inputs may be any that keep to these rules, and one draw needn't show every extreme that they name: `pair_chan`: row p holds channels i < j with j - i at most 125, and i lies in the block of 32 channels numbered p // 128.
All inputs are finite; a program needn't handle non-finite values. No bound on the sum of `alive` on one device may be relied on, other than what follows from the above.
Results may differ from the reference program's by a relative error of at most 0.014.
Values may be sent and summed in bfloat16 or wider, within the bound.
A program may use at most 384 MiB of HBM per device.

```python
import math
import jax
import jax.numpy as jnp
from jax import lax

FREQ = 4096
SAMP = 8192
BAND = 64
LAGS = 512
REACH = 125
CH_DEV = 32
PAIR_DEV = 128
CHANNELS = 1024
SEGS = 16
PAIRS = 4096


def draw_pair_chan(key, part):
    key = jax.random.fold_in(key, 7)
    key_first, key_second = jax.random.split(key)
    row_index = jnp.arange(PAIRS, dtype=jnp.int32)
    owner = row_index // PAIR_DEV
    first = owner * CH_DEV + jax.random.randint(key_first, (PAIRS,), 0, CH_DEV - 1, dtype=jnp.int32)
    distance = jax.random.randint(key_second, (PAIRS,), 1, REACH + 1, dtype=jnp.int32)
    second = jnp.minimum(first + distance, CHANNELS - 1)
    first = first.at[0].set(0)
    second = second.at[0].set(1)
    first = first.at[PAIRS - 1].set(CHANNELS - 2)
    second = second.at[PAIRS - 1].set(CHANNELS - 1)
    return jnp.stack([first, second], axis=1)


def place_ends(drawn, key, smallest, high):
    dims = drawn.shape
    spot = [jax.random.randint(jax.random.fold_in(key, axis), (), 0, dims[axis]) for axis in range(len(dims))]
    drawn = drawn.at[tuple(spot)].set(smallest)
    longest = dims.index(max(dims))
    spot[longest] = (spot[longest] + 1) % dims[longest]
    return drawn.at[tuple(spot)].set(high)


def steps_of(stream_key, shape, shards, low, top_value):
    def one(dim, parts):
        heights = jax.random.uniform(jax.random.fold_in(jax.random.fold_in(stream_key, 6), dim), (parts,), jnp.float32, low / len(shards), top_value / len(shards))
        return jnp.repeat(jnp.exp(heights), shape[dim] // parts).reshape((-1,) + (1,) * (len(shape) - dim - 1))

    loudness = one(*shards[0])
    for cut in shards[1:]:
        loudness = loudness * one(*cut)
    return loudness


def normal_values(stream_key, extent, spread, bound, pieces=(), held_as=jnp.bfloat16):
    gain = steps_of(stream_key, extent, pieces, -0.22, 0.18) if pieces else 1.0
    values = jax.random.normal(stream_key, extent, jnp.float32) * spread * gain
    return jnp.minimum(jnp.maximum(values, -bound), bound).astype(held_as)


def setup_inputs(seed: int = 0) -> dict:
    splits = jax.random.split(jax.random.key(seed), 5)
    return {
        "traces": normal_values(splits[0], (CHANNELS, SEGS, SAMP), 1.0, 6.0, ((0, 32), (1, 4))),
        "alive": place_ends((jax.random.randint(splits[1], (CHANNELS,), 0, 16) < 15).astype(jnp.int32), jax.random.fold_in(splits[1], 1), 0, 1),
        "pair_chan": draw_pair_chan(jax.random.fold_in(splits[4], 71), 0),
        "lag_window": place_ends(jax.random.randint(splits[3], (PAIRS,), 4, LAGS // 2 + 1), jax.random.fold_in(splits[3], 1), 4, (LAGS // 2 + 1) - 1).astype(jnp.int32),
    }


eps_whiten = 1e-06

def dft_table(first_bin, width):
    time_index = jnp.arange(SAMP, dtype=jnp.int32)[:, None]
    bin_index = first_bin + jnp.arange(width, dtype=jnp.int32)[None, :]
    phase = time_index * bin_index % SAMP
    angle = phase.astype(jnp.float32) * (2.0 * math.pi / SAMP)
    return jnp.concatenate([jnp.cos(angle), -jnp.sin(angle)], axis=1).astype(jnp.bfloat16)

def band_scale(real_part, imag_part):
    magnitude = jnp.sqrt(real_part * real_part + imag_part * imag_part)
    level = magnitude.reshape(magnitude.shape[0], -1, BAND).mean(axis=2)
    return jnp.repeat(1.0 / (level + eps_whiten), BAND, axis=1)

def lag_table():
    freq_index = jnp.arange(FREQ, dtype=jnp.int32)[:, None]
    lag_shift = (jnp.arange(LAGS, dtype=jnp.int32) - LAGS // 2) % SAMP
    phase = freq_index * lag_shift[None, :] % SAMP
    angle = phase.astype(jnp.float32) * (2.0 * math.pi / SAMP)
    return jnp.concatenate([jnp.cos(angle), -jnp.sin(angle)], axis=0)

def reference(traces, alive, pair_chan, lag_window):
    table = dft_table(0, FREQ).astype(jnp.float32)
    trace_rows = traces.reshape(CHANNELS * SEGS, SAMP).astype(jnp.float32)
    spectrum = jnp.dot(trace_rows, table, precision=lax.Precision.HIGHEST, preferred_element_type=jnp.float32)
    real_part = spectrum[:, :FREQ]
    imag_part = spectrum[:, FREQ:]
    scale = band_scale(real_part, imag_part)
    live_rows = jnp.repeat(alive.astype(jnp.float32), SEGS)[:, None]
    whitened = jnp.concatenate([real_part * scale * live_rows, imag_part * scale * live_rows], axis=1)
    whitened = whitened.astype(jnp.bfloat16).reshape(CHANNELS, SEGS, 2 * FREQ)
    first_side = jnp.take(whitened, pair_chan[:, 0], axis=0).astype(jnp.float32)
    second_side = jnp.take(whitened, pair_chan[:, 1], axis=0).astype(jnp.float32)
    first_real, first_imag = (first_side[..., :FREQ], first_side[..., FREQ:])
    second_real, second_imag = (second_side[..., :FREQ], second_side[..., FREQ:])
    factor = 1.0 / math.sqrt(SEGS * FREQ)
    cross_real = lax.optimization_barrier(jnp.sum(first_real * second_real + first_imag * second_imag, axis=1)) * factor
    cross_imag = lax.optimization_barrier(jnp.sum(first_imag * second_real - first_real * second_imag, axis=1)) * factor
    cross = jnp.concatenate([cross_real, cross_imag], axis=1)
    lagged = jnp.dot(cross, lag_table(), precision=lax.Precision.HIGHEST, preferred_element_type=jnp.float32)
    lag_value = jnp.abs(jnp.arange(LAGS, dtype=jnp.int32) - LAGS // 2)
    keep = lag_value[None, :] <= lag_window[:, None]
    return jnp.where(keep, lagged, jnp.zeros_like(lagged))
```

```python
import functools
import math

import jax
import jax.numpy as jnp
import numpy as np
from jax import lax
from jax.experimental import pallas as pl
from jax.experimental.pallas import tpu as pltpu
from jax.sharding import PartitionSpec as P

FREQ = 4096
SAMP = 8192
BAND = 64
LAGS = 512
UNITS = 32
ROW = 4
CH = 32
SEG = 4
EPS = 1e-06


def unit_bins():
    u = np.arange(UNITS)[:, None]
    lane = np.arange(128)[None, :]
    low = np.where(lane < 64, u, np.where(u == 0, 32, 64 - u))
    return low + 64 * (lane % 64)


def second_table():
    bins = unit_bins()[:, None, :]
    t2 = np.arange(128)[None, :, None]
    angle = 2.0 * np.pi * ((t2 * bins) % SAMP) / SAMP
    c, s = np.cos(angle), np.sin(angle)
    first = np.arange(128)[None, None, :] < 64
    unit0 = np.arange(UNITS)[:, None, None] == 0
    sign = np.where(first, 1.0, -1.0)
    rr = np.where(unit0, np.where(first, c, 0.0), c)
    ri = np.where(unit0, np.where(first, -s, 0.0), -s)
    ir = np.where(unit0, np.where(first, 0.0, c), sign * s)
    ii = np.where(unit0, np.where(first, 0.0, -s), sign * c)
    top = np.concatenate([rr, ri], axis=2)
    bottom = np.concatenate([ir, ii], axis=2)
    return np.concatenate([top, bottom], axis=1).astype(jnp.bfloat16)


def lag_table():
    bins = unit_bins()[:, :, None].astype(np.int64)
    tau = np.arange(LAGS)[None, None, :] - LAGS // 2
    angle = 2.0 * np.pi * ((bins * tau) % SAMP) / SAMP
    return (np.concatenate([np.cos(angle), -np.sin(angle)], axis=1) / 256.0).astype(jnp.bfloat16)


def real_dft(values):
    n = len(values)
    if n == 1:
        return [values[0]], [None]
    if n == 2:
        return [values[0] + values[1], values[0] - values[1]], [None, None]
    er, ei = real_dft(values[0::2])
    odr, odi = real_dft(values[1::2])
    half, quarter = n // 2, n // 4
    re, im = [None] * (half + 1), [None] * (half + 1)
    re[0], re[half] = er[0] + odr[0], er[0] - odr[0]
    re[quarter], im[quarter] = er[quarter], -odr[quarter]
    for k in range(1, quarter):
        c, s = math.cos(2 * math.pi * k / n), math.sin(2 * math.pi * k / n)
        if 8 * k == n:
            pr, pi = (odr[k] + odi[k]) * c, (odi[k] - odr[k]) * c
        else:
            pr, pi = odr[k] * c + odi[k] * s, odi[k] * c - odr[k] * s
        re[k], im[k] = er[k] + pr, ei[k] + pi
        re[half - k], im[half - k] = er[k] - pr, pi - ei[k]
    return re, im


def whiten_kernel(x_ref, live_ref, table_hbm, out_ref, mid, spec, level, table, sem):
    fetch = pltpu.make_async_copy(table_hbm, table, sem)
    fetch.start()

    def first_stage(block, carry):
        start = pl.multiple_of(block * 16, 16)
        for part in range(2):
            values = [
                x_ref[pl.ds(start, 16), pl.ds(128 * t, 128)].astype(jnp.float32)[8 * part : 8 * part + 8]
                for t in range(64)
            ]
            re, im = real_dft(values)
            rows = pl.ds(pl.multiple_of(start + 8 * part, 8), 8)
            mid[0, rows, 0:128] = re[0]
            mid[0, rows, 128:256] = re[32]
            for k in range(1, 32):
                mid[k, rows, 0:128] = re[k]
                mid[k, rows, 128:256] = im[k]
        return carry

    lax.fori_loop(0, 8, first_stage, 0)
    fetch.wait()
    level[...] = jnp.zeros_like(level)

    def second_stage(u, carry):
        got = jnp.dot(mid[u].astype(jnp.bfloat16), table[u], preferred_element_type=jnp.float32)
        re, im = got[:, :128], got[:, 128:]
        spec[u, 0] = re
        spec[u, 1] = im
        level[...] += jnp.sqrt(re * re + im * im)
        return carry

    lax.fori_loop(0, UNITS, second_stage, 0, unroll=4)
    total = level[...]
    level[...] = 1.0 / ((total + pltpu.roll(total, 64, 1)) * (1.0 / BAND) + EPS)

    def third_stage(u, carry):
        for s in range(SEG):
            scale = level[pl.ds(s, CH, stride=SEG), :] * live_ref[...]
            for half in range(2):
                cols = pl.ds(128 * half, 128)
                got = spec[u, half, pl.ds(s, CH, stride=SEG), :] * scale
                out_ref[u, s, :, cols] = got.astype(jnp.bfloat16)
        return carry

    lax.fori_loop(0, UNITS, third_stage, 0, unroll=2)


def whiten(rows, live, table):
    return pl.pallas_call(
        whiten_kernel,
        out_shape=jax.ShapeDtypeStruct((UNITS, SEG, CH, 256), jnp.bfloat16),
        in_specs=[
            pl.BlockSpec(memory_space=pltpu.VMEM),
            pl.BlockSpec(memory_space=pltpu.VMEM),
            pl.BlockSpec(memory_space=pl.ANY),
        ],
        out_specs=pl.BlockSpec(memory_space=pltpu.VMEM),
        scratch_shapes=[
            pltpu.VMEM((UNITS, 128, 256), jnp.float32),
            pltpu.VMEM((UNITS, 2, 128, 128), jnp.float32),
            pltpu.VMEM((128, 128), jnp.float32),
            pltpu.VMEM((UNITS, 256, 256), jnp.bfloat16),
            pltpu.SemaphoreType.DMA,
        ],
        compiler_params=pltpu.CompilerParams(vmem_limit_bytes=48 * 2**20),
    )(rows, live, table)


def pair_kernel(place, idx_ref, g_ref, h_ref, lag_ref, out_ref, first_pick, second_pick):
    unit = pl.program_id(0)
    late = unit // 4

    @pl.when(unit % 4 == 0)
    def _():
        lanes = lax.broadcasted_iota(jnp.int32, (512, 128), 1)
        i = idx_ref[0, :, 0:1]
        j = idx_ref[0, :, 1:2]
        first_pick[...] = jnp.where(lanes == i, 1.0, 0.0).astype(jnp.bfloat16)
        second_pick[:, 0:128] = jnp.where(lanes == j, 1.0, 0.0).astype(jnp.bfloat16)
        second_pick[:, 128:256] = jnp.where(lanes + 128 == j, 1.0, 0.0).astype(jnp.bfloat16)
        out_ref[...] = jnp.zeros_like(out_ref)

    def side(ref, s):
        return jnp.concatenate([ref[b, 0, s] for b in range(ROW)], axis=0)

    def work(near, far):
        cross_re = cross_im = None
        for s in range(SEG):
            own, other = side(near, s), side(far, s)
            a = jnp.dot(first_pick[...], own, preferred_element_type=jnp.float32)
            b = jnp.dot(second_pick[...], jnp.concatenate([own, other], axis=0), preferred_element_type=jnp.float32)
            ar, ai, br, bi = a[:, :128], a[:, 128:], b[:, :128], b[:, 128:]
            re, im = ar * br + ai * bi, ai * br - ar * bi
            cross_re = re if cross_re is None else cross_re + re
            cross_im = im if cross_im is None else cross_im + im
        cross = jnp.concatenate([cross_re, cross_im], axis=1).astype(jnp.bfloat16)
        out_ref[0] += jnp.dot(cross, lag_ref[0], preferred_element_type=jnp.float32)

    @pl.when(late == 0)
    def _():
        work(g_ref, h_ref)

    @pl.when(late == 1)
    def _():
        work(h_ref, g_ref)


def pair_partials(place, idx, g, h, lag):
    spectra = pl.BlockSpec((ROW, 1, SEG, CH, 256), lambda u, y: (0, u, 0, 0, 0))
    return pl.pallas_call(
        pair_kernel,
        out_shape=jax.ShapeDtypeStruct((2, 512, LAGS), jnp.float32),
        grid_spec=pltpu.PrefetchScalarGridSpec(
            num_scalar_prefetch=1,
            grid=(8,),
            in_specs=[
                pl.BlockSpec((1, 512, 2), lambda u, y: (u // 4, 0, 0)),
                spectra,
                spectra,
                pl.BlockSpec((1, 256, LAGS), lambda u, y: (8 * y[0] + u, 0, 0)),
            ],
            out_specs=pl.BlockSpec((1, 512, LAGS), lambda u, y: (u // 4, 0, 0)),
            scratch_shapes=[pltpu.VMEM((512, 128), jnp.bfloat16), pltpu.VMEM((512, 256), jnp.bfloat16)],
        ),
        compiler_params=pltpu.CompilerParams(vmem_limit_bytes=48 * 2**20),
    )(place, idx, g, h, lag)


def body(traces, alive, pair_chan, lag_window):
    n = lax.axis_size("chan")
    me = lax.axis_index("chan")
    row, y = me // ROW, me % ROW
    rows = n // ROW
    groups = [[r * ROW + k for k in range(ROW)] for r in range(rows)]
    live = jnp.broadcast_to(alive.astype(jnp.float32)[:, None], (CH, 128))
    spectra = whiten(traces.reshape(CH * SEG, SAMP), live, jnp.asarray(second_table()))
    g = lax.all_to_all(
        spectra.reshape(ROW, 8, SEG, CH, 256), "chan", split_axis=0, concat_axis=0, axis_index_groups=groups
    )
    back = [(i, (i - ROW) % n) for i in range(n)]
    ahead = [(i, (i + ROW) % n) for i in range(n)]
    h = jnp.concatenate(
        [lax.ppermute(g[:, :4], "chan", back), lax.ppermute(g[:, 4:], "chan", ahead)], axis=1
    )
    all_pairs = lax.all_gather(pair_chan, "chan", tiled=True)
    before = (row + rows - 1) % rows
    idx = jnp.stack(
        [
            lax.dynamic_slice_in_dim(all_pairs, row * 512, 512) - row * 128,
            lax.dynamic_slice_in_dim(all_pairs, before * 512, 512) - before * 128,
        ]
    )
    partial = pair_partials(y[None], idx, g, h, jnp.asarray(lag_table()))
    partial = partial.astype(jnp.bfloat16).reshape(2, ROW, SEG, 32, LAGS)
    partial = lax.psum_scatter(partial, "chan", scatter_dimension=1, axis_index_groups=groups)
    partial = lax.psum_scatter(partial, "seg", scatter_dimension=1)
    lagged = (partial[0] + lax.ppermute(partial[1], "chan", back)).astype(jnp.float32)
    lag_value = jnp.abs(jnp.arange(LAGS, dtype=jnp.int32) - LAGS // 2)
    keep = lag_value[None, :] <= lag_window[:, None]
    return jnp.where(keep, lagged, jnp.zeros_like(lagged))


def solution(mesh):
    in_specs = (P("chan", "seg", None), P("chan"), P("chan", None), P(("chan", "seg")))
    out_specs = P(("chan", "seg"), None)
    return jax.shard_map(body, mesh=mesh, in_specs=in_specs, out_specs=out_specs, check_vma=False)
```

```python
import functools
import math

import jax
import jax.numpy as jnp
import numpy as np
from jax import lax
from jax.experimental import pallas as pl
from jax.experimental.pallas import tpu as pltpu
from jax.sharding import PartitionSpec as P

FREQ = 4096
SAMP = 8192
BAND = 64
LAGS = 512
UNITS = 32
ROW = 4
CH = 32
SEG = 4
EPS = 1e-06
AHEAD = 3
DELAY = 3
MESH = pl.DeviceIdType.MESH


def unit_bins():
    u = np.arange(UNITS)[:, None]
    lane = np.arange(128)[None, :]
    low = np.where(lane < 64, u, np.where(u == 0, 32, 64 - u))
    return low + 64 * (lane % 64)


def second_table():
    bins = unit_bins()[:, None, :]
    t2 = np.arange(128)[None, :, None]
    angle = 2.0 * np.pi * ((t2 * bins) % SAMP) / SAMP
    c, s = np.cos(angle), np.sin(angle)
    first = np.arange(128)[None, None, :] < 64
    unit0 = np.arange(UNITS)[:, None, None] == 0
    sign = np.where(first, 1.0, -1.0)
    rr = np.where(unit0, np.where(first, c, 0.0), c)
    ri = np.where(unit0, np.where(first, -s, 0.0), -s)
    ir = np.where(unit0, np.where(first, 0.0, c), sign * s)
    ii = np.where(unit0, np.where(first, 0.0, -s), sign * c)
    top = np.concatenate([rr, ri], axis=2)
    bottom = np.concatenate([ir, ii], axis=2)
    return np.concatenate([top, bottom], axis=1).astype(jnp.bfloat16)


def lag_table():
    bins = unit_bins()[:, :, None].astype(np.int64)
    tau = np.arange(LAGS)[None, None, :] - LAGS // 2
    angle = 2.0 * np.pi * ((bins * tau) % SAMP) / SAMP
    return (np.concatenate([np.cos(angle), -np.sin(angle)], axis=1) / 256.0).astype(jnp.bfloat16)


def real_dft(values):
    n = len(values)
    if n == 1:
        return [values[0]], [None]
    if n == 2:
        return [values[0] + values[1], values[0] - values[1]], [None, None]
    er, ei = real_dft(values[0::2])
    odr, odi = real_dft(values[1::2])
    half, quarter = n // 2, n // 4
    re, im = [None] * (half + 1), [None] * (half + 1)
    re[0], re[half] = er[0] + odr[0], er[0] - odr[0]
    re[quarter], im[quarter] = er[quarter], -odr[quarter]
    for k in range(1, quarter):
        c, s = math.cos(2 * math.pi * k / n), math.sin(2 * math.pi * k / n)
        if 8 * k == n:
            pr, pi = (odr[k] + odi[k]) * c, (odi[k] - odr[k]) * c
        else:
            pr, pi = odr[k] * c + odi[k] * s, odi[k] * c - odr[k] * s
        re[k], im[k] = er[k] + pr, ei[k] + pi
        re[half - k], im[half - k] = er[k] - pr, pi - ei[k]
    return re, im


def whiten_kernel(x_ref, live_ref, table_hbm, out_ref, mid, spec, level, table, sem):
    fetch = pltpu.make_async_copy(table_hbm, table, sem)
    fetch.start()

    def first_stage(block, carry):
        start = pl.multiple_of(block * 16, 16)
        for part in range(2):
            values = [
                x_ref[pl.ds(start, 16), pl.ds(128 * t, 128)].astype(jnp.float32)[8 * part : 8 * part + 8]
                for t in range(64)
            ]
            re, im = real_dft(values)
            rows = pl.ds(pl.multiple_of(start + 8 * part, 8), 8)
            mid[0, rows, 0:128] = re[0]
            mid[0, rows, 128:256] = re[32]
            for k in range(1, 32):
                mid[k, rows, 0:128] = re[k]
                mid[k, rows, 128:256] = im[k]
        return carry

    lax.fori_loop(0, 8, first_stage, 0)
    fetch.wait()
    level[...] = jnp.zeros_like(level)

    def second_stage(u, carry):
        got = jnp.dot(mid[u].astype(jnp.bfloat16), table[u], preferred_element_type=jnp.float32)
        re, im = got[:, :128], got[:, 128:]
        spec[u, 0] = re
        spec[u, 1] = im
        level[...] += jnp.sqrt(re * re + im * im)
        return carry

    lax.fori_loop(0, UNITS, second_stage, 0, unroll=4)
    total = level[...]
    level[...] = 1.0 / ((total + pltpu.roll(total, 64, 1)) * (1.0 / BAND) + EPS)

    def third_stage(u, carry):
        for s in range(SEG):
            scale = level[pl.ds(s, CH, stride=SEG), :] * live_ref[...]
            for half in range(2):
                cols = pl.ds(128 * half, 128)
                got = spec[u, half, pl.ds(s, CH, stride=SEG), :] * scale
                out_ref[u, s, :, cols] = got.astype(jnp.bfloat16)
        return carry

    lax.fori_loop(0, UNITS, third_stage, 0, unroll=2)


def whiten(rows, live, table):
    return pl.pallas_call(
        whiten_kernel,
        out_shape=jax.ShapeDtypeStruct((UNITS, SEG, CH, 256), jnp.bfloat16),
        in_specs=[
            pl.BlockSpec(memory_space=pltpu.VMEM),
            pl.BlockSpec(memory_space=pltpu.VMEM),
            pl.BlockSpec(memory_space=pl.ANY),
        ],
        out_specs=pl.BlockSpec(memory_space=pltpu.VMEM),
        scratch_shapes=[
            pltpu.VMEM((UNITS, 128, 256), jnp.float32),
            pltpu.VMEM((UNITS, 2, 128, 128), jnp.float32),
            pltpu.VMEM((128, 128), jnp.float32),
            pltpu.VMEM((UNITS, 256, 256), jnp.bfloat16),
            pltpu.SemaphoreType.DMA,
        ],
        compiler_params=pltpu.CompilerParams(vmem_limit_bytes=48 * 2**20),
    )(rows, live, table)


def exchange_kernel(
    rows, pair_ref, window_ref, w_ref, lag_hbm, out_ref,
    both, lag, idx, first_pick, second_pick, total, half_out, half_in, piece, got,
    y_send, y_recv, x_send, x_recv, idx_send, idx_recv, half_send, half_recv, sum_send, sum_recv, local,
):
    me, seg = lax.axis_index("chan"), lax.axis_index("seg")
    row, y = me // ROW, me % ROW
    zh, core = seg // 2, seg % 2
    before, after = (row + rows - 1) % rows, (row + 1) % rows
    mine = y * 2 + zh

    def at(r, q):
        return (r * ROW + q // 2, (q % 2) * 2 + core)

    def remote(src, dst, send, recv, device):
        return pltpu.make_async_remote_copy(
            src_ref=src, dst_ref=dst, send_sem=send, recv_sem=recv, device_id=device, device_id_type=MESH
        )

    sibling = (me, zh * 2 + 1 - core)
    barrier = pltpu.get_barrier_semaphore()

    def greet(device):
        pl.semaphore_signal(barrier, inc=1, device_id=device, device_id_type=MESH)

    greet(sibling)
    for k in range(8):
        if k:
            greet(at(row, (mine + k) % 8))
        greet(at(before, (mine + k) % 8))
        greet(at(after, (mine + k) % 8))
    pl.semaphore_wait(barrier, 24)

    fetch = pltpu.make_async_copy(lag_hbm.at[pl.ds(8 * y, 8)], lag, local.at[0])
    keep_own = pltpu.make_async_copy(w_ref.at[y], both.at[0, :, :, y], local.at[1])

    def y_copy(d, u):
        to = (y + d) % ROW
        return remote(
            w_ref.at[to, u], both.at[0, u, :, y], y_send.at[d - 1, u], y_recv.at[d - 1, u], (row * ROW + to, seg)
        )

    def y_arrival(d, u):
        source = (y + ROW - d) % ROW
        return remote(
            w_ref.at[y, u], both.at[0, u, :, source], y_send.at[d - 1, u], y_recv.at[d - 1, u],
            (row * ROW + source, seg),
        )

    def x_copy(u):
        to = (row + rows - 1 + 2 * (u // 4)) % rows
        return remote(both.at[0, u], both.at[1, u], x_send.at[u], x_recv.at[u], (to * ROW + y, seg))

    def unit_of(step):
        return (step % 2) * 4 + step // 2

    def start_y(step):
        for d in (2, 1, 3):
            y_copy(d, unit_of(step)).start()

    for step in range(AHEAD):
        start_y(step)
    keep_own.start()
    fetch.start()

    own_idx = [pltpu.make_async_copy(pair_ref, idx.at[y], local.at[2])]
    sends, waits = [], []
    for d in range(1, ROW):
        sends.append(
            remote(pair_ref, idx.at[y], idx_send.at[d], idx_recv.at[d], (row * ROW + (y + d) % ROW, seg))
        )
        waits.append(
            remote(pair_ref, idx.at[(y + ROW - d) % ROW], idx_send.at[d], idx_recv.at[d],
                   (row * ROW + (y + d) % ROW, seg))
        )
    for d in range(ROW):
        sends.append(
            remote(pair_ref, idx.at[ROW + y], idx_send.at[4 + d], idx_recv.at[4 + d],
                   (after * ROW + (y + d) % ROW, seg))
        )
        waits.append(
            remote(pair_ref, idx.at[ROW + (y + ROW - d) % ROW], idx_send.at[4 + d], idx_recv.at[4 + d],
                   (after * ROW + (y + d) % ROW, seg))
        )
    for copy in own_idx + sends:
        copy.start()
    total[...] = jnp.zeros_like(total)
    own_idx[0].wait()
    for copy in sends:
        copy.wait_send()
    for copy in waits:
        copy.wait_recv()

    channel = lax.broadcasted_iota(jnp.int32, (128, 128), 0)

    def make_picks(slot, carry):
        side = slot // ROW
        base = jnp.where(side == 0, row, before) * (ROW * CH)
        at_rows = pl.ds(pl.multiple_of((slot % ROW) * 128, 128), 128)

        def picks(which, shift):
            hit = channel + (base + shift) == idx[slot, which : which + 1, :]
            return jnp.where(hit, 1.0, 0.0).T.astype(jnp.bfloat16)

        first_pick[side, at_rows, :] = picks(0, 0)
        second_pick[side, at_rows, 0:128] = picks(1, 0)
        second_pick[side, at_rows, 128:256] = picks(1, 128)
        return carry

    lax.fori_loop(0, 8, make_picks, 0)
    keep_own.wait()
    fetch.wait()

    def correlate(u):
        late = u // 4
        cross_re = cross_im = None
        for s in range(SEG):
            near = both[late, u, s].reshape(128, 256)
            far = both[1 - late, u, s].reshape(128, 256)
            a = jnp.dot(first_pick[late], near, preferred_element_type=jnp.float32)
            b = jnp.dot(
                second_pick[late], jnp.concatenate([near, far], axis=0), preferred_element_type=jnp.float32
            )
            ar, ai, br, bi = a[:, :128], a[:, 128:], b[:, :128], b[:, 128:]
            re, im = ar * br + ai * bi, ai * br - ar * bi
            cross_re = re if cross_re is None else cross_re + re
            cross_im = im if cross_im is None else cross_im + im
        cross = jnp.concatenate([cross_re, cross_im], axis=1).astype(jnp.bfloat16)
        total[late] += jnp.dot(cross, lag[u], preferred_element_type=jnp.float32)

    def advance(step, carry):
        @pl.when(step + AHEAD < 8)
        def _():
            start_y(step + AHEAD)

        @pl.when(step < 8)
        def _():
            u = unit_of(step)
            for d in (1, 3, 2):
                y_arrival(d, u).wait_recv()
            x_copy(u).start()

        @pl.when(step >= DELAY)
        def _():
            u = unit_of(step - DELAY)
            x_copy(u).wait_recv()
            correlate(u)

        return carry

    lax.fori_loop(0, 8 + DELAY, advance, 0)

    def sent(u, carry):
        for d in (1, 2, 3):
            y_copy(d, u).wait_send()
        x_copy(u).wait_send()
        return carry

    lax.fori_loop(0, 8, sent, 0)

    def rows_of(q, c):
        return pl.ds(pl.multiple_of(q * 64 + c * 32, 32), 32)

    def half_copy(side):
        return remote(half_out.at[side], half_in.at[side], half_send.at[side], half_recv.at[side], sibling)

    for side in range(2):
        def pack(q, carry, side=side):
            half_out[side, q] = total[side, rows_of(q, 1 - core), :].astype(jnp.bfloat16)
            return carry

        lax.fori_loop(0, 8, pack, 0)
        half_copy(side).start()

    def sum_copy(side, k):
        to = row if side == 0 else before
        q = (mine + k) % 8
        return remote(piece.at[side, q], got.at[side, k], sum_send.at[side, k], sum_recv.at[side, k], at(to, q))

    for side in range(2):
        half_copy(side).wait_recv()

        def combine(q, carry, side=side):
            value = total[side, rows_of(q, core), :] + half_in[side, q].astype(jnp.float32)
            piece[side, q] = value.astype(jnp.bfloat16)
            return carry

        lax.fori_loop(0, 8, combine, 0)
        for k in range(1 - side, 8):
            sum_copy(side, k).start()
    for side in range(2):
        half_copy(side).wait_send()

    result = piece[0, mine].astype(jnp.float32)
    for side in range(2):
        for k in range(1 - side, 8):
            sum_copy(side, k).wait_recv()
            result = result + got[side, k].astype(jnp.float32)
    diagonal = lax.broadcasted_iota(jnp.int32, (32, 32), 0) == lax.broadcasted_iota(jnp.int32, (32, 32), 1)
    widest = jnp.sum(jnp.where(diagonal, window_ref[...].astype(jnp.float32), 0.0), axis=1, keepdims=True)
    lags = jnp.abs(lax.broadcasted_iota(jnp.int32, (32, LAGS), 1) - LAGS // 2).astype(jnp.float32)
    out_ref[...] = jnp.where(lags <= widest, result, 0.0)
    for side in range(2):
        for k in range(1 - side, 8):
            sum_copy(side, k).wait_send()


def exchange(rows, pairs, window, spectra, lag):
    dma = pltpu.SemaphoreType.DMA
    vmem = pl.BlockSpec(memory_space=pltpu.VMEM)
    pieces = pltpu.VMEM((2, 8, 32, LAGS), jnp.bfloat16)
    return pl.pallas_call(
        functools.partial(exchange_kernel, rows),
        out_shape=jax.ShapeDtypeStruct((32, LAGS), jnp.float32),
        in_specs=[vmem, vmem, vmem, pl.BlockSpec(memory_space=pl.ANY)],
        out_specs=vmem,
        scratch_shapes=[
            pltpu.VMEM((2, 8, SEG, ROW, CH, 256), jnp.bfloat16),
            pltpu.VMEM((8, 256, LAGS), jnp.bfloat16),
            pltpu.VMEM((8, 2, 128), jnp.int32),
            pltpu.VMEM((2, 512, 128), jnp.bfloat16),
            pltpu.VMEM((2, 512, 256), jnp.bfloat16),
            pltpu.VMEM((2, 512, LAGS), jnp.float32),
            pieces,
            pieces,
            pieces,
            pieces,
            dma((3, 8)),
            dma((3, 8)),
            dma((8,)),
            dma((8,)),
            dma((8,)),
            dma((8,)),
            dma((2,)),
            dma((2,)),
            dma((2, 8)),
            dma((2, 8)),
            dma((3,)),
        ],
        compiler_params=pltpu.CompilerParams(
            collective_id=0, has_side_effects=True, vmem_limit_bytes=48 * 2**20
        ),
    )(pairs, window, spectra, lag)


def body(traces, alive, pair_chan, lag_window):
    rows = lax.axis_size("chan") // ROW
    live = jnp.broadcast_to(alive.astype(jnp.float32)[:, None], (CH, 128))
    spectra = whiten(traces.reshape(CH * SEG, SAMP), live, jnp.asarray(second_table()))
    return exchange(
        rows, pair_chan.T, lag_window[None], spectra.reshape(ROW, 8, SEG, CH, 256), jnp.asarray(lag_table())
    )


def solution(mesh):
    in_specs = (P("chan", "seg", None), P("chan"), P("chan", None), P(("chan", "seg")))
    out_specs = P(("chan", "seg"), None)
    return jax.shard_map(body, mesh=mesh, in_specs=in_specs, out_specs=out_specs, check_vma=False)
```

```python
import functools
import math

import jax
import jax.numpy as jnp
import numpy as np
from jax import lax
from jax.experimental import pallas as pl
from jax.experimental.pallas import tpu as pltpu
from jax.sharding import PartitionSpec as P

FREQ = 4096
SAMP = 8192
BAND = 64
LAGS = 512
UNITS = 32
ROW = 4
CH = 32
SEG = 4
EPS = 1e-06
AHEAD = 4
DELAY = 4
PICKS = 6
MESH = pl.DeviceIdType.MESH


def unit_bins():
    u = np.arange(UNITS)[:, None]
    lane = np.arange(128)[None, :]
    low = np.where(lane < 64, u, np.where(u == 0, 32, 64 - u))
    return low + 64 * (lane % 64)


def second_table():
    bins = unit_bins()[:, None, :]
    t2 = np.arange(128)[None, :, None]
    angle = 2.0 * np.pi * ((t2 * bins) % SAMP) / SAMP
    c, s = np.cos(angle), np.sin(angle)
    first = np.arange(128)[None, None, :] < 64
    unit0 = np.arange(UNITS)[:, None, None] == 0
    sign = np.where(first, 1.0, -1.0)
    rr = np.where(unit0, np.where(first, c, 0.0), c)
    ri = np.where(unit0, np.where(first, -s, 0.0), -s)
    ir = np.where(unit0, np.where(first, 0.0, c), sign * s)
    ii = np.where(unit0, np.where(first, 0.0, -s), sign * c)
    top = np.concatenate([rr, ri], axis=2)
    bottom = np.concatenate([ir, ii], axis=2)
    return np.concatenate([top, bottom], axis=1).astype(jnp.bfloat16)


def lag_table():
    bins = unit_bins()[:, :, None].astype(np.int64)
    tau = np.arange(LAGS)[None, None, :] - LAGS // 2
    angle = 2.0 * np.pi * ((bins * tau) % SAMP) / SAMP
    return (np.concatenate([np.cos(angle), -np.sin(angle)], axis=1) / 256.0).astype(jnp.bfloat16)


def real_dft(values):
    n = len(values)
    if n == 1:
        return [values[0]], [None]
    if n == 2:
        return [values[0] + values[1], values[0] - values[1]], [None, None]
    er, ei = real_dft(values[0::2])
    odr, odi = real_dft(values[1::2])
    half, quarter = n // 2, n // 4
    re, im = [None] * (half + 1), [None] * (half + 1)
    re[0], re[half] = er[0] + odr[0], er[0] - odr[0]
    re[quarter], im[quarter] = er[quarter], -odr[quarter]
    for k in range(1, quarter):
        c, s = math.cos(2 * math.pi * k / n), math.sin(2 * math.pi * k / n)
        if 8 * k == n:
            pr, pi = (odr[k] + odi[k]) * c, (odi[k] - odr[k]) * c
        else:
            pr, pi = odr[k] * c + odi[k] * s, odi[k] * c - odr[k] * s
        re[k], im[k] = er[k] + pr, ei[k] + pi
        re[half - k], im[half - k] = er[k] - pr, pi - ei[k]
    return re, im


def kernel(
    rows, traces_hbm, alive_ref, pair_ref, window_ref, table_hbm, lag_hbm, out_ref,
    x, mid, spec, level, table, w,
    both, lag, idx, first_pick, second_pick, total, half_out, half_in, piece, got,
    y_send, y_recv, x_send, x_recv, idx_send, idx_recv, half_send, half_recv, sum_send, sum_recv, local,
):
    me, seg = lax.axis_index("chan"), lax.axis_index("seg")
    row, y = me // ROW, me % ROW
    zh, core = seg // 2, seg % 2
    before, after = (row + rows - 1) % rows, (row + 1) % rows
    mine = y * 2 + zh

    def at(r, q):
        return (r * ROW + q // 2, (q % 2) * 2 + core)

    def remote(src, dst, send, recv, device):
        return pltpu.make_async_remote_copy(
            src_ref=src, dst_ref=dst, send_sem=send, recv_sem=recv, device_id=device, device_id_type=MESH
        )

    sibling = (me, zh * 2 + 1 - core)
    barrier = pltpu.get_barrier_semaphore()

    def greet(device):
        pl.semaphore_signal(barrier, inc=1, device_id=device, device_id_type=MESH)

    load = [
        pltpu.make_async_copy(traces_hbm.at[pl.ds(16 * h, 16)], x.at[pl.ds(16 * h, 16)], local.at[h]) for h in range(2)
    ]
    load[0].start()
    fetch_table = pltpu.make_async_copy(table_hbm, table, local.at[2])
    fetch_table.start()
    load[1].start()
    fetch_lag = pltpu.make_async_copy(lag_hbm.at[pl.ds(8 * y, 8)], lag, local.at[3])
    fetch_lag.start()

    greet(sibling)
    for k in range(8):
        if k:
            greet(at(row, (mine + k) % 8))
        greet(at(before, (mine + k) % 8))
        greet(at(after, (mine + k) % 8))

    def keep_own(h):
        return pltpu.make_async_copy(w.at[h, y], both.at[0, h, :, :, y], local.at[4 + h])

    def column(values):
        n = values.shape[1]
        diagonal = lax.broadcasted_iota(jnp.int32, (n, n), 0) == lax.broadcasted_iota(jnp.int32, (n, n), 1)
        return jnp.sum(jnp.where(diagonal, values.astype(jnp.float32), 0.0), axis=1, keepdims=True)

    live = column(alive_ref[...])

    def whiten(h):
        load[h].wait()

        def first_stage(block, carry):
            channels = pl.ds(16 * h + 2 * block, 2)
            values = [
                x[channels, :, pl.ds(128 * t, 128)].astype(jnp.float32).reshape(8, 128) for t in range(64)
            ]
            re, im = real_dft(values)
            at_rows = pl.ds(pl.multiple_of(8 * block, 8), 8)
            mid[0, at_rows, 0:128] = re[0]
            mid[0, at_rows, 128:256] = re[32]
            for k in range(1, 32):
                mid[k, at_rows, 0:128] = re[k]
                mid[k, at_rows, 128:256] = im[k]
            return carry

        lax.fori_loop(0, 8, first_stage, 0)
        if h == 0:
            fetch_table.wait()
        level[...] = jnp.zeros_like(level)

        def second_stage(u, carry):
            result = jnp.dot(mid[u].astype(jnp.bfloat16), table[u], preferred_element_type=jnp.float32)
            re, im = result[:, :128], result[:, 128:]
            spec[u, 0] = re
            spec[u, 1] = im
            level[...] += jnp.sqrt(re * re + im * im)
            return carry

        lax.fori_loop(0, UNITS, second_stage, 0, unroll=4)
        sums = level[...]
        level[...] = 1.0 / ((sums + pltpu.roll(sums, 64, 1)) * (1.0 / BAND) + EPS)
        scales = [level[pl.ds(s, 16, stride=SEG), :] * live[16 * h : 16 * h + 16] for s in range(SEG)]

        def third_stage(u, carry):
            for s in range(SEG):
                for part in range(2):
                    value = spec[u, part, pl.ds(s, 16, stride=SEG), :] * scales[s]
                    w[h, u // 8, u % 8, s, :, pl.ds(128 * part, 128)] = value.astype(jnp.bfloat16)
            return carry

        lax.fori_loop(0, UNITS, third_stage, 0, unroll=2)

    def y_copy(d, h, u):
        to = (y + d) % ROW
        return remote(
            w.at[h, to, u], both.at[0, h, u, :, y], y_send.at[d - 1, h, u], y_recv.at[d - 1, h, u], (row * ROW + to, seg)
        )

    def y_arrival(d, h, u):
        source = (y + ROW - d) % ROW
        return remote(
            w.at[h, y, u], both.at[0, h, u, :, source], y_send.at[d - 1, h, u], y_recv.at[d - 1, h, u],
            (row * ROW + source, seg),
        )

    def x_copy(h, u):
        to = (row + rows - 1 + 2 * (u // 4)) % rows
        return remote(both.at[0, h, u], both.at[1, h, u], x_send.at[h, u], x_recv.at[h, u], (to * ROW + y, seg))

    def unit_of(step):
        return (step % 2) * 4 + (step % 8) // 2

    def start_y(step):
        for d in (2, 1, 3):
            y_copy(d, step // 8, unit_of(step)).start()

    own_idx = pltpu.make_async_copy(pair_ref, idx.at[y], local.at[6])
    own_idx.start()

    def idx_copy(k, slot):
        r = row if k < ROW else after
        return remote(pair_ref, idx.at[slot], idx_send.at[k], idx_recv.at[k], (r * ROW + (y + k) % ROW, seg))

    whiten(0)
    pl.semaphore_wait(barrier, 24)
    for step in range(AHEAD):
        start_y(step)
    for k in range(1, 8):
        idx_copy(k, y + (0 if k < ROW else ROW)).start()
    keep_own(0).start()
    whiten(1)
    keep_own(1).start()
    total[...] = jnp.zeros_like(total)

    channel_row = lax.broadcasted_iota(jnp.int32, (128, 128), 0)
    channel = ((channel_row // 16) % ROW) * CH + (channel_row // 64) * 16 + channel_row % 16

    def make_picks(slot, carry):
        side = slot // ROW
        base = jnp.where(side == 0, row, before) * (ROW * CH)
        at_rows = pl.ds(pl.multiple_of((slot % ROW) * 128, 128), 128)

        def picks(which, shift):
            hit = channel + (base + shift) == idx[slot, which : which + 1, :]
            return jnp.where(hit, 1.0, 0.0).T.astype(jnp.bfloat16)

        first_pick[side, at_rows, :] = picks(0, 0)
        second_pick[side, at_rows, 0:128] = picks(1, 0)
        second_pick[side, at_rows, 128:256] = picks(1, 128)
        return carry

    def spectra(side, u, s):
        return [both[side, h, u, s].reshape(64, 256) for h in range(2)]

    def correlate(u):
        late = u // 4
        cross_re = cross_im = None
        for s in range(SEG):
            near = jnp.concatenate(spectra(late, u, s), axis=0)
            far = jnp.concatenate(spectra(1 - late, u, s), axis=0)
            a = jnp.dot(first_pick[late], near, preferred_element_type=jnp.float32)
            b = jnp.dot(
                second_pick[late], jnp.concatenate([near, far], axis=0), preferred_element_type=jnp.float32
            )
            ar, ai, br, bi = a[:, :128], a[:, 128:], b[:, :128], b[:, 128:]
            re, im = ar * br + ai * bi, ai * br - ar * bi
            cross_re = re if cross_re is None else cross_re + re
            cross_im = im if cross_im is None else cross_im + im
        cross = jnp.concatenate([cross_re, cross_im], axis=1).astype(jnp.bfloat16)
        total[late] += jnp.dot(cross, lag[u], preferred_element_type=jnp.float32)

    def advance(step, carry):
        @pl.when(step + AHEAD < 16)
        def _():
            start_y(step + AHEAD)

        @pl.when(step % 8 == 0)
        def _():
            @pl.when(step == 0)
            def _():
                keep_own(0).wait()

            @pl.when(step == 8)
            def _():
                keep_own(1).wait()

        @pl.when(step < 16)
        def _():
            h, u = step // 8, unit_of(step)
            for d in (1, 3, 2):
                y_arrival(d, h, u).wait_recv()
            x_copy(h, u).start()

        @pl.when(step == PICKS)
        def _():
            own_idx.wait()
            for k in range(1, 8):
                idx_copy(k, (y + ROW - k % ROW) % ROW + (0 if k < ROW else ROW)).wait_recv()
            lax.fori_loop(0, 8, make_picks, 0)
            fetch_lag.wait()

        @pl.when(step >= 8 + DELAY)
        def _():
            u = unit_of(step - DELAY)
            for h in range(2):
                x_copy(h, u).wait_recv()
            correlate(u)

        return carry

    lax.fori_loop(0, 16 + DELAY, advance, 0)

    def rows_of(q, c):
        return pl.ds(pl.multiple_of(q * 64 + c * 32, 32), 32)

    def half_copy(side):
        return remote(half_out.at[side], half_in.at[side], half_send.at[side], half_recv.at[side], sibling)

    for side in range(2):
        def pack(q, carry, side=side):
            half_out[side, q] = total[side, rows_of(q, 1 - core), :].astype(jnp.bfloat16)
            return carry

        lax.fori_loop(0, 8, pack, 0)
        half_copy(side).start()

    def sum_copy(side, k):
        to = row if side == 0 else before
        q = (mine + k) % 8
        return remote(piece.at[side, q], got.at[side, k], sum_send.at[side, k], sum_recv.at[side, k], at(to, q))

    for side in range(2):
        half_copy(side).wait_recv()

        def combine(q, carry, side=side):
            value = total[side, rows_of(q, core), :] + half_in[side, q].astype(jnp.float32)
            piece[side, q] = value.astype(jnp.bfloat16)
            return carry

        lax.fori_loop(0, 8, combine, 0)
        for k in range(1 - side, 8):
            sum_copy(side, k).start()

    def sent(u, carry):
        for h in range(2):
            for d in (1, 2, 3):
                y_copy(d, h, u).wait_send()
            x_copy(h, u).wait_send()
        return carry

    lax.fori_loop(0, 8, sent, 0)
    for k in range(1, 8):
        idx_copy(k, y + (0 if k < ROW else ROW)).wait_send()
    for side in range(2):
        half_copy(side).wait_send()

    result = piece[0, mine].astype(jnp.float32)
    for side in range(2):
        for k in range(1 - side, 8):
            sum_copy(side, k).wait_recv()
            result = result + got[side, k].astype(jnp.float32)
    widest = column(window_ref[...])
    lags = jnp.abs(lax.broadcasted_iota(jnp.int32, (32, LAGS), 1) - LAGS // 2).astype(jnp.float32)
    out_ref[...] = jnp.where(lags <= widest, result, 0.0)
    for side in range(2):
        for k in range(1 - side, 8):
            sum_copy(side, k).wait_send()


def body(traces, alive, pair_chan, lag_window):
    rows = lax.axis_size("chan") // ROW
    dma = pltpu.SemaphoreType.DMA
    vmem = pl.BlockSpec(memory_space=pltpu.VMEM)
    hbm = pl.BlockSpec(memory_space=pl.ANY)
    pieces = pltpu.VMEM((2, 8, 32, LAGS), jnp.bfloat16)
    return pl.pallas_call(
        functools.partial(kernel, rows),
        out_shape=jax.ShapeDtypeStruct((32, LAGS), jnp.float32),
        in_specs=[hbm, vmem, vmem, vmem, hbm, hbm],
        out_specs=vmem,
        scratch_shapes=[
            pltpu.VMEM((CH, SEG, SAMP), jnp.bfloat16),
            pltpu.VMEM((UNITS, 64, 256), jnp.float32),
            pltpu.VMEM((UNITS, 2, 64, 128), jnp.float32),
            pltpu.VMEM((64, 128), jnp.float32),
            pltpu.VMEM((UNITS, 256, 256), jnp.bfloat16),
            pltpu.VMEM((2, ROW, 8, SEG, 16, 256), jnp.bfloat16),
            pltpu.VMEM((2, 2, 8, SEG, ROW, 16, 256), jnp.bfloat16),
            pltpu.VMEM((8, 256, LAGS), jnp.bfloat16),
            pltpu.VMEM((8, 2, 128), jnp.int32),
            pltpu.VMEM((2, 512, 128), jnp.bfloat16),
            pltpu.VMEM((2, 512, 256), jnp.bfloat16),
            pltpu.VMEM((2, 512, LAGS), jnp.float32),
            pieces,
            pieces,
            pieces,
            pieces,
            dma((3, 2, 8)),
            dma((3, 2, 8)),
            dma((2, 8)),
            dma((2, 8)),
            dma((8,)),
            dma((8,)),
            dma((2,)),
            dma((2,)),
            dma((2, 8)),
            dma((2, 8)),
            dma((7,)),
        ],
        compiler_params=pltpu.CompilerParams(
            collective_id=0, has_side_effects=True, vmem_limit_bytes=48 * 2**20
        ),
    )(
        traces,
        alive[None],
        pair_chan.T,
        lag_window[None],
        jnp.asarray(second_table()),
        jnp.asarray(lag_table()),
    )


def solution(mesh):
    in_specs = (P("chan", "seg", None), P("chan"), P("chan", None), P(("chan", "seg")))
    out_specs = P(("chan", "seg"), None)
    return jax.shard_map(body, mesh=mesh, in_specs=in_specs, out_specs=out_specs, check_vma=False)
```

```python
import functools
import math

import jax
import jax.numpy as jnp
import numpy as np
from jax import lax
from jax.experimental import pallas as pl
from jax.experimental.pallas import tpu as pltpu
from jax.sharding import PartitionSpec as P

FREQ = 4096
SAMP = 8192
BAND = 64
LAGS = 512
UNITS = 32
ROW = 4
CH = 32
SEG = 4
EPS = 1e-06
AHEAD = 3
DELAY = 2
PICKS = 4
MESH = pl.DeviceIdType.MESH


def unit_bins():
    u = np.arange(UNITS)[:, None]
    lane = np.arange(128)[None, :]
    low = np.where(lane < 64, u, np.where(u == 0, 32, 64 - u))
    return low + 64 * (lane % 64)


def second_table():
    bins = unit_bins()[:, None, :]
    t2 = np.arange(128)[None, :, None]
    angle = 2.0 * np.pi * ((t2 * bins) % SAMP) / SAMP
    c, s = np.cos(angle), np.sin(angle)
    first = np.arange(128)[None, None, :] < 64
    unit0 = np.arange(UNITS)[:, None, None] == 0
    sign = np.where(first, 1.0, -1.0)
    rr = np.where(unit0, np.where(first, c, 0.0), c)
    ri = np.where(unit0, np.where(first, -s, 0.0), -s)
    ir = np.where(unit0, np.where(first, 0.0, c), sign * s)
    ii = np.where(unit0, np.where(first, 0.0, -s), sign * c)
    top = np.concatenate([rr, ri], axis=2)
    bottom = np.concatenate([ir, ii], axis=2)
    return np.concatenate([top, bottom], axis=1).astype(jnp.bfloat16)


def lag_table():
    bins = unit_bins()[:, :, None].astype(np.int64)
    tau = np.arange(LAGS)[None, None, :] - LAGS // 2
    angle = 2.0 * np.pi * ((bins * tau) % SAMP) / SAMP
    return (np.concatenate([np.cos(angle), -np.sin(angle)], axis=1) / 256.0).astype(jnp.bfloat16)


def real_dft(values):
    n = len(values)
    if n == 1:
        return [values[0]], [None]
    if n == 2:
        return [values[0] + values[1], values[0] - values[1]], [None, None]
    er, ei = real_dft(values[0::2])
    odr, odi = real_dft(values[1::2])
    half, quarter = n // 2, n // 4
    re, im = [None] * (half + 1), [None] * (half + 1)
    re[0], re[half] = er[0] + odr[0], er[0] - odr[0]
    re[quarter], im[quarter] = er[quarter], -odr[quarter]
    for k in range(1, quarter):
        c, s = math.cos(2 * math.pi * k / n), math.sin(2 * math.pi * k / n)
        if 8 * k == n:
            pr, pi = (odr[k] + odi[k]) * c, (odi[k] - odr[k]) * c
        else:
            pr, pi = odr[k] * c + odi[k] * s, odi[k] * c - odr[k] * s
        re[k], im[k] = er[k] + pr, ei[k] + pi
        re[half - k], im[half - k] = er[k] - pr, pi - ei[k]
    return re, im


def kernel(
    rows, traces_hbm, alive_hbm, pair_hbm, window_hbm, table_hbm, lag_hbm, out_ref,
    alive_ref, pair_ref, window_ref, x, mid, spec, level, table, w,
    both, lag, idx, first_pick, second_pick, total, piece, got,
    y_send, y_recv, own_send, own_recv, x_send, x_recv, rest_send, rest_recv,
    idx_send, idx_recv, sum_send, sum_recv, local,
):
    me, seg = lax.axis_index("chan"), lax.axis_index("seg")
    row, y = me // ROW, me % ROW
    zh, core = seg // 2, seg % 2
    before, after = (row + rows - 1) % rows, (row + 1) % rows
    mine = y * 2 + zh
    pair_row = (row + rows - core) % rows
    my_segs = pl.ds(SEG * core, SEG)

    def at(r, q, c):
        return (r * ROW + q // 2, (q % 2) * 2 + c)

    def remote(src, dst, send, recv, device):
        return pltpu.make_async_remote_copy(
            src_ref=src, dst_ref=dst, send_sem=send, recv_sem=recv, device_id=device, device_id_type=MESH
        )

    sibling = (me, zh * 2 + 1 - core)
    barrier = pltpu.get_barrier_semaphore()

    def greet(device):
        pl.semaphore_signal(barrier, inc=1, device_id=device, device_id_type=MESH)

    load = [
        pltpu.make_async_copy(traces_hbm.at[pl.ds(16 * h, 16)], x.at[pl.ds(16 * h, 16)], local.at[h]) for h in range(2)
    ]
    small = [
        pltpu.make_async_copy(src, dst, local.at[7 + k])
        for k, (src, dst) in enumerate(((alive_hbm, alive_ref), (pair_hbm, pair_ref), (window_hbm, window_ref)))
    ]
    load[0].start()
    for copy in small:
        copy.start()
    fetch_table = pltpu.make_async_copy(table_hbm, table, local.at[2])
    fetch_table.start()
    load[1].start()
    fetch_lag = pltpu.make_async_copy(lag_hbm.at[pl.ds(8 * y + 4 * core, 4)], lag, local.at[3])
    fetch_lag.start()

    greet(sibling)
    for k in range(8):
        for c in range(2):
            if k:
                greet(at(row, (mine + k) % 8, c))
            greet(at(before, (mine + k) % 8, c))
            greet(at(after, (mine + k) % 8, c))

    def column(values):
        n = values.shape[1]
        diagonal = lax.broadcasted_iota(jnp.int32, (n, n), 0) == lax.broadcasted_iota(jnp.int32, (n, n), 1)
        return jnp.sum(jnp.where(diagonal, values.astype(jnp.float32), 0.0), axis=1, keepdims=True)

    for copy in small:
        copy.wait()
    live = column(alive_ref[...])

    def whiten(h):
        load[h].wait()

        def first_stage(block, carry):
            channels = pl.ds(16 * h + 2 * block, 2)
            values = [
                x[channels, :, pl.ds(128 * t, 128)].astype(jnp.float32).reshape(8, 128) for t in range(64)
            ]
            re, im = real_dft(values)
            at_rows = pl.ds(pl.multiple_of(8 * block, 8), 8)
            mid[0, at_rows, 0:128] = re[0]
            mid[0, at_rows, 128:256] = re[32]
            for k in range(1, 32):
                mid[k, at_rows, 0:128] = re[k]
                mid[k, at_rows, 128:256] = im[k]
            return carry

        lax.fori_loop(0, 8, first_stage, 0)
        if h == 0:
            fetch_table.wait()
        level[...] = jnp.zeros_like(level)

        def second_stage(u, carry):
            result = jnp.dot(mid[u].astype(jnp.bfloat16), table[u], preferred_element_type=jnp.float32)
            re, im = result[:, :128], result[:, 128:]
            spec[u, 0] = re
            spec[u, 1] = im
            level[...] += jnp.sqrt(re * re + im * im)
            return carry

        lax.fori_loop(0, UNITS, second_stage, 0, unroll=4)
        sums = level[...]
        level[...] = 1.0 / ((sums + pltpu.roll(sums, 64, 1)) * (1.0 / BAND) + EPS)
        scales = [level[pl.ds(s, 16, stride=SEG), :] * live[16 * h : 16 * h + 16] for s in range(SEG)]

        def third_stage(u, carry):
            for s in range(SEG):
                for part in range(2):
                    value = spec[u, part, pl.ds(s, 16, stride=SEG), :] * scales[s]
                    w[h, u // 8, u % 8, s, :, pl.ds(128 * part, 128)] = value.astype(jnp.bfloat16)
            return carry

        lax.fori_loop(0, UNITS, third_stage, 0, unroll=2)

    def keep_own(h):
        return pltpu.make_async_copy(
            w.at[h, y, pl.ds(4 * core, 4)], both.at[0, h, :, my_segs, 0], local.at[4 + h]
        )

    def give_own(h):
        return remote(
            w.at[h, y, pl.ds(4 * (1 - core), 4)], both.at[0, h, :, my_segs, 0], own_send.at[h], own_recv.at[h], sibling
        )

    def take_own(h):
        other = pl.ds(SEG * (1 - core), SEG)
        return remote(w.at[h, y, pl.ds(0, 4)], both.at[0, h, :, other, 0], own_send.at[h], own_recv.at[h], sibling)

    def y_copy(d, h, u, side):
        to = (y + d) % ROW
        return remote(
            w.at[h, to, 4 * side + u], both.at[0, h, u, my_segs, d], y_send.at[side, d - 1, h, u],
            y_recv.at[core, d - 1, h, u], (row * ROW + to, zh * 2 + side),
        )

    def y_arrival(d, h, u, c):
        return remote(
            w.at[h, y, u], both.at[0, h, u, pl.ds(SEG * c, SEG), d], y_send.at[0, d - 1, h, u],
            y_recv.at[c, d - 1, h, u], sibling,
        )

    def x_copy(h, u, side):
        to = before if side == 0 else after
        return remote(
            w.at[h, y, 4 * side + u], both.at[1, h, u, my_segs, 0], x_send.at[side, h, u], x_recv.at[core, h, u],
            (to * ROW + y, zh * 2 + side),
        )

    def x_arrival(h, u, c):
        return remote(
            w.at[h, y, u], both.at[1, h, u, pl.ds(SEG * c, SEG), 0], x_send.at[0, h, u], x_recv.at[c, h, u], sibling
        )

    def rest_copy(h, u):
        to = (row + rows - 1 + 2 * core) % rows
        others = pl.ds(1, 3)
        return remote(
            both.at[0, h, u, :, others], both.at[1, h, u, :, others], rest_send.at[h, u], rest_recv.at[h, u],
            (to * ROW + y, seg),
        )

    def start_y(step):
        h, u = step // 4, step % 4
        for d in (2, 1, 3):
            for side in range(2):
                y_copy(d, h, u, side).start()
        for side in range(2):
            x_copy(h, u, side).start()

    def idx_copy(k, slot):
        r = (row + core) % rows
        return remote(pair_ref, idx.at[slot], idx_send.at[k], idx_recv.at[k], (r * ROW + (y + k) % ROW, seg))

    own_idx = pltpu.make_async_copy(pair_ref, idx.at[y], local.at[6])

    whiten(0)
    pl.semaphore_wait(barrier, 47)
    for step in range(AHEAD):
        start_y(step)
    for k in range(1, ROW):
        idx_copy(k, y).start()

    @pl.when(core == 0)
    def _():
        own_idx.start()

    @pl.when(core == 1)
    def _():
        idx_copy(0, y).start()

    give_own(0).start()
    keep_own(0).start()
    whiten(1)
    give_own(1).start()
    keep_own(1).start()
    total[...] = jnp.zeros_like(total)

    channel_row = lax.broadcasted_iota(jnp.int32, (128, 128), 0)
    source_y = (y + ROW - (channel_row // 16) % ROW) % ROW
    channel = pair_row * (ROW * CH) + source_y * CH + (channel_row // 64) * 16 + channel_row % 16

    def make_picks(slot, carry):
        at_rows = pl.ds(pl.multiple_of(slot * 128, 128), 128)

        def picks(which, shift):
            hit = channel + shift == idx[slot, which : which + 1, :]
            return jnp.where(hit, 1.0, 0.0).T.astype(jnp.bfloat16)

        first_pick[at_rows, :] = picks(0, 0)
        second_pick[at_rows, 0:128] = picks(1, 0)
        second_pick[at_rows, 128:256] = picks(1, 128)
        return carry

    def spectra(side, u, s):
        return [both[side, h, u, s].reshape(64, 256) for h in range(2)]

    def correlate(u):
        cross_re = cross_im = None
        for s in range(2 * SEG):
            near = jnp.concatenate(spectra(core, u, s), axis=0)
            far = jnp.concatenate(spectra(1 - core, u, s), axis=0)
            a = jnp.dot(first_pick[...], near, preferred_element_type=jnp.float32)
            b = jnp.dot(second_pick[...], jnp.concatenate([near, far], axis=0), preferred_element_type=jnp.float32)
            ar, ai, br, bi = a[:, :128], a[:, 128:], b[:, :128], b[:, 128:]
            re, im = ar * br + ai * bi, ai * br - ar * bi
            cross_re = re if cross_re is None else cross_re + re
            cross_im = im if cross_im is None else cross_im + im
        cross = jnp.concatenate([cross_re, cross_im], axis=1).astype(jnp.bfloat16)
        total[...] += jnp.dot(cross, lag[u], preferred_element_type=jnp.float32)

    def advance(step, carry):
        @pl.when(step + AHEAD < 8)
        def _():
            start_y(step + AHEAD)

        @pl.when(step < 8)
        def _():
            h, u = step // 4, step % 4
            for d in (1, 3, 2):
                for c in range(2):
                    y_arrival(d, h, u, c).wait_recv()
            rest_copy(h, u).start()

        @pl.when(step == PICKS)
        def _():
            @pl.when(core == 0)
            def _():
                own_idx.wait()

            @pl.when(core == 1)
            def _():
                idx_copy(0, y).wait_recv()

            for k in range(1, ROW):
                idx_copy(k, (y + ROW - k) % ROW).wait_recv()
            lax.fori_loop(0, ROW, make_picks, 0)
            fetch_lag.wait()
            for h in range(2):
                keep_own(h).wait()
                take_own(h).wait_recv()

        @pl.when(step >= 4 + DELAY)
        def _():
            u = (step - DELAY) % 4
            for h in range(2):
                for c in range(2):
                    x_arrival(h, u, c).wait_recv()
                rest_copy(h, u).wait_recv()
            correlate(u)

        return carry

    lax.fori_loop(0, 8 + DELAY, advance, 0)

    def sum_copy(k, c):
        q = (mine + k) % 8
        return remote(piece.at[q, c], got.at[core, k], sum_send.at[k, c], sum_recv.at[core, k], at(pair_row, q, c))

    def sum_arrival(side, k):
        return remote(piece.at[0, 0], got.at[side, k], sum_send.at[k, 0], sum_recv.at[side, k], sibling)

    for k in (4, 5, 3, 7, 1, 6, 2, 0):
        q = (mine + k) % 8
        for c in range(2):
            piece[q, c] = total[pl.ds(pl.multiple_of(q * 64 + c * 32, 32), 32), :].astype(jnp.bfloat16)
            if k or c:
                sum_copy(k, c).start()
    stays = core == 0

    @pl.when(stays)
    def _():
        got[0, 0] = piece[mine, 0]

    @pl.when(core == 1)
    def _():
        sum_copy(0, 0).start()

    def sent(u, carry):
        for h in range(2):
            for side in range(2):
                for d in (1, 2, 3):
                    y_copy(d, h, u, side).wait_send()
                x_copy(h, u, side).wait_send()
            rest_copy(h, u).wait_send()
        return carry

    lax.fori_loop(0, 4, sent, 0)
    for h in range(2):
        give_own(h).wait_send()
    for k in range(1, ROW):
        idx_copy(k, y).wait_send()

    @pl.when(core == 1)
    def _():
        idx_copy(0, y).wait_send()
        sum_arrival(0, 0).wait_recv()

    widest = column(window_ref[...])
    lags = jnp.abs(lax.broadcasted_iota(jnp.int32, (32, LAGS), 1) - LAGS // 2).astype(jnp.float32)
    for side, k in [(0, k) for k in range(1, 8)] + [(1, k) for k in range(8)]:
        sum_arrival(side, k).wait_recv()
    result = jnp.zeros((32, LAGS), jnp.float32)
    for side in range(2):
        for k in range(8):
            result = result + got[side, k].astype(jnp.float32)
    out_ref[...] = jnp.where(lags <= widest, result, 0.0)
    for k in range(8):
        for c in range(2):
            if k or c:
                sum_copy(k, c).wait_send()

    @pl.when(core == 1)
    def _():
        sum_copy(0, 0).wait_send()


def body(traces, alive, pair_chan, lag_window):
    rows = lax.axis_size("chan") // ROW
    dma = pltpu.SemaphoreType.DMA
    hbm = pl.BlockSpec(memory_space=pl.ANY)
    return pl.pallas_call(
        functools.partial(kernel, rows),
        out_shape=jax.ShapeDtypeStruct((32, LAGS), jnp.float32),
        in_specs=[hbm] * 6,
        out_specs=pl.BlockSpec(memory_space=pltpu.VMEM),
        scratch_shapes=[
            pltpu.VMEM((1, CH), jnp.int32),
            pltpu.VMEM((2, 128), jnp.int32),
            pltpu.VMEM((1, 32), jnp.int32),
            pltpu.VMEM((CH, SEG, SAMP), jnp.bfloat16),
            pltpu.VMEM((UNITS, 64, 256), jnp.float32),
            pltpu.VMEM((UNITS, 2, 64, 128), jnp.float32),
            pltpu.VMEM((64, 128), jnp.float32),
            pltpu.VMEM((UNITS, 256, 256), jnp.bfloat16),
            pltpu.VMEM((2, ROW, 8, SEG, 16, 256), jnp.bfloat16),
            pltpu.VMEM((2, 2, 4, 2 * SEG, ROW, 16, 256), jnp.bfloat16),
            pltpu.VMEM((4, 256, LAGS), jnp.bfloat16),
            pltpu.VMEM((ROW, 2, 128), jnp.int32),
            pltpu.VMEM((512, 128), jnp.bfloat16),
            pltpu.VMEM((512, 256), jnp.bfloat16),
            pltpu.VMEM((512, LAGS), jnp.float32),
            pltpu.VMEM((8, 2, 32, LAGS), jnp.bfloat16),
            pltpu.VMEM((2, 8, 32, LAGS), jnp.bfloat16),
            dma((2, 3, 2, 4)),
            dma((2, 3, 2, 4)),
            dma((2,)),
            dma((2,)),
            dma((2, 2, 4)),
            dma((2, 2, 4)),
            dma((2, 4)),
            dma((2, 4)),
            dma((ROW,)),
            dma((ROW,)),
            dma((8, 2)),
            dma((2, 8)),
            dma((10,)),
        ],
        compiler_params=pltpu.CompilerParams(
            collective_id=0, has_side_effects=True, vmem_limit_bytes=60 * 2**20
        ),
    )(
        traces,
        alive[None],
        pair_chan.T,
        lag_window[None],
        jnp.asarray(second_table()),
        jnp.asarray(lag_table()),
    )


def solution(mesh):
    in_specs = (P("chan", "seg", None), P("chan"), P("chan", None), P(("chan", "seg")))
    out_specs = P(("chan", "seg"), None)
    return jax.shard_map(body, mesh=mesh, in_specs=in_specs, out_specs=out_specs, check_vma=False)
```

```python
import functools
import math

import jax
import jax.numpy as jnp
import numpy as np
from jax import lax
from jax.experimental import pallas as pl
from jax.experimental.pallas import tpu as pltpu
from jax.sharding import PartitionSpec as P

FREQ = 4096
SAMP = 8192
BAND = 64
LAGS = 512
UNITS = 32
ROW = 4
CH = 32
SEG = 4
EPS = 1e-06
AHEAD = 4
DELAY = 4
PICKS = 8
MESH = pl.DeviceIdType.MESH


def unit_bins():
    u = np.arange(UNITS)[:, None]
    lane = np.arange(128)[None, :]
    low = np.where(lane < 64, u, np.where(u == 0, 32, 64 - u))
    return low + 64 * (lane % 64)


def second_table():
    bins = unit_bins()[:, None, :]
    t2 = np.arange(128)[None, :, None]
    angle = 2.0 * np.pi * ((t2 * bins) % SAMP) / SAMP
    c, s = np.cos(angle), np.sin(angle)
    first = np.arange(128)[None, None, :] < 64
    unit0 = np.arange(UNITS)[:, None, None] == 0
    sign = np.where(first, 1.0, -1.0)
    rr = np.where(unit0, np.where(first, c, 0.0), c)
    ri = np.where(unit0, np.where(first, -s, 0.0), -s)
    ir = np.where(unit0, np.where(first, 0.0, c), sign * s)
    ii = np.where(unit0, np.where(first, 0.0, -s), sign * c)
    top = np.concatenate([rr, ri], axis=2)
    bottom = np.concatenate([ir, ii], axis=2)
    return np.concatenate([top, bottom], axis=1).astype(jnp.bfloat16)


def lag_table():
    bins = unit_bins()[:, :, None].astype(np.int64)
    tau = np.arange(LAGS)[None, None, :] - LAGS // 2
    angle = 2.0 * np.pi * ((bins * tau) % SAMP) / SAMP
    return (np.concatenate([np.cos(angle), -np.sin(angle)], axis=1) / 256.0).astype(jnp.bfloat16)


def real_dft(values):
    n = len(values)
    if n == 1:
        return [values[0]], [None]
    if n == 2:
        return [values[0] + values[1], values[0] - values[1]], [None, None]
    er, ei = real_dft(values[0::2])
    odr, odi = real_dft(values[1::2])
    half, quarter = n // 2, n // 4
    re, im = [None] * (half + 1), [None] * (half + 1)
    re[0], re[half] = er[0] + odr[0], er[0] - odr[0]
    re[quarter], im[quarter] = er[quarter], -odr[quarter]
    for k in range(1, quarter):
        c, s = math.cos(2 * math.pi * k / n), math.sin(2 * math.pi * k / n)
        if 8 * k == n:
            pr, pi = (odr[k] + odi[k]) * c, (odi[k] - odr[k]) * c
        else:
            pr, pi = odr[k] * c + odi[k] * s, odi[k] * c - odr[k] * s
        re[k], im[k] = er[k] + pr, ei[k] + pi
        re[half - k], im[half - k] = er[k] - pr, pi - ei[k]
    return re, im


def kernel(
    rows, traces_hbm, alive_hbm, pair_hbm, window_hbm, table_hbm, lag_hbm, out_ref,
    alive_ref, pair_ref, window_ref, x, mid, spec, level, table, w,
    both, lag, idx, first_pick, second_pick, total, piece, got, row_got, row_sum, late_sum,
    y_send, y_recv, own_send, own_recv, x_send, x_recv, rest_send, rest_recv,
    idx_send, idx_recv, sum_send, sum_recv, row_send, row_recv, late_send, late_recv, local,
):
    me, seg = lax.axis_index("chan"), lax.axis_index("seg")
    row, y = me // ROW, me % ROW
    zh, core = seg // 2, seg % 2
    before, after = (row + rows - 1) % rows, (row + 1) % rows
    mine = y * 2 + zh
    pair_row = (row + rows - core) % rows
    my_segs = pl.ds(SEG * core, SEG)

    def at(r, q, c):
        return (r * ROW + q // 2, (q % 2) * 2 + c)

    def remote(src, dst, send, recv, device):
        return pltpu.make_async_remote_copy(
            src_ref=src, dst_ref=dst, send_sem=send, recv_sem=recv, device_id=device, device_id_type=MESH
        )

    sibling = (me, zh * 2 + 1 - core)
    barrier = pltpu.get_barrier_semaphore()

    def greet(device):
        pl.semaphore_signal(barrier, inc=1, device_id=device, device_id_type=MESH)

    load = [
        pltpu.make_async_copy(traces_hbm.at[pl.ds(16 * h, 16)], x.at[pl.ds(16 * h, 16)], local.at[h]) for h in range(2)
    ]
    small = [
        pltpu.make_async_copy(src, dst, local.at[7 + k])
        for k, (src, dst) in enumerate(((alive_hbm, alive_ref), (pair_hbm, pair_ref), (window_hbm, window_ref)))
    ]
    load[0].start()
    for copy in small:
        copy.start()
    fetch_table = pltpu.make_async_copy(table_hbm, table, local.at[2])
    fetch_table.start()
    load[1].start()
    fetch_lag = pltpu.make_async_copy(lag_hbm.at[pl.ds(8 * y + 4 * core, 4)], lag, local.at[3])
    fetch_lag.start()

    greet(sibling)
    for k in range(1, 8):
        for c in range(2):
            greet(at(row, (mine + k) % 8, c))
    for r in (before, after):
        for c in range(2):
            greet((r * ROW + y, zh * 2 + c))

        @pl.when(core == 1)
        def _(r=r):
            for k in range(1, ROW):
                greet((r * ROW + (y + k) % ROW, seg))

    def column(values):
        n = values.shape[1]
        diagonal = lax.broadcasted_iota(jnp.int32, (n, n), 0) == lax.broadcasted_iota(jnp.int32, (n, n), 1)
        return jnp.sum(jnp.where(diagonal, values.astype(jnp.float32), 0.0), axis=1, keepdims=True)

    for copy in small:
        copy.wait()
    live = column(alive_ref[...])

    def whiten(h):
        load[h].wait()

        def first_stage(block, carry):
            channels = pl.ds(16 * h + 2 * block, 2)
            values = [
                x[channels, :, pl.ds(128 * t, 128)].astype(jnp.float32).reshape(8, 128) for t in range(64)
            ]
            re, im = real_dft(values)
            at_rows = pl.ds(pl.multiple_of(8 * block, 8), 8)
            mid[0, at_rows, 0:128] = re[0]
            mid[0, at_rows, 128:256] = re[32]
            for k in range(1, 32):
                mid[k, at_rows, 0:128] = re[k]
                mid[k, at_rows, 128:256] = im[k]
            return carry

        lax.fori_loop(0, 8, first_stage, 0)
        if h == 0:
            fetch_table.wait()
        level[...] = jnp.zeros_like(level)

        def second_stage(u, carry):
            result = jnp.dot(mid[u].astype(jnp.bfloat16), table[u], preferred_element_type=jnp.float32)
            re, im = result[:, :128], result[:, 128:]
            spec[u, 0] = re
            spec[u, 1] = im
            level[...] += jnp.sqrt(re * re + im * im)
            return carry

        lax.fori_loop(0, UNITS, second_stage, 0, unroll=8)
        sums = level[...]
        level[...] = 1.0 / ((sums + pltpu.roll(sums, 64, 1)) * (1.0 / BAND) + EPS)
        scales = [level[pl.ds(s, 16, stride=SEG), :] * live[16 * h : 16 * h + 16] for s in range(SEG)]

        def third_stage(u, carry):
            for s in range(SEG):
                for part in range(2):
                    value = spec[u, part, pl.ds(s, 16, stride=SEG), :] * scales[s]
                    w[h, u // 8, u % 8, s, :, pl.ds(128 * part, 128)] = value.astype(jnp.bfloat16)
            return carry

        lax.fori_loop(0, UNITS, third_stage, 0, unroll=2)

    def keep_own(h):
        return pltpu.make_async_copy(
            w.at[h, y, pl.ds(4 * core, 4)], both.at[0, h, :, my_segs, 0], local.at[4 + h]
        )

    def give_own(h):
        return remote(
            w.at[h, y, pl.ds(4 * (1 - core), 4)], both.at[0, h, :, my_segs, 0], own_send.at[h], own_recv.at[h], sibling
        )

    def take_own(h):
        other = pl.ds(SEG * (1 - core), SEG)
        return remote(w.at[h, y, pl.ds(0, 4)], both.at[0, h, :, other, 0], own_send.at[h], own_recv.at[h], sibling)

    def y_copy(d, h, u, side):
        to = (y + d) % ROW
        return remote(
            w.at[h, to, 4 * side + u], both.at[0, h, u, my_segs, d], y_send.at[side, d - 1, h, u],
            y_recv.at[core, d - 1, h, u], (row * ROW + to, zh * 2 + side),
        )

    def y_arrival(d, h, u, c):
        return remote(
            w.at[h, y, u], both.at[0, h, u, pl.ds(SEG * c, SEG), d], y_send.at[0, d - 1, h, u],
            y_recv.at[c, d - 1, h, u], sibling,
        )

    def x_copy(h, u, side):
        to = (row + rows - 1 + 2 * side) % rows
        return remote(
            w.at[h, y, 4 * side + u], both.at[1, h, u, my_segs, 0], x_send.at[side, h, u], x_recv.at[core, h, u],
            (to * ROW + y, zh * 2 + side),
        )

    def x_arrival(h, u, c):
        return remote(
            w.at[h, y, u], both.at[1, h, u, pl.ds(SEG * c, SEG), 0], x_send.at[0, h, u], x_recv.at[c, h, u], sibling
        )

    def rest_copy(d, h, u):
        to = (row + rows - 1 + 2 * core) % rows
        return remote(
            both.at[0, h, u, :, d], both.at[1, h, u, :, d], rest_send.at[d - 1, h, u], rest_recv.at[d - 1, h, u],
            (to * ROW + y, seg),
        )

    def item(step):
        first = ((step % 2 == 0) & (step >= 2)) | (step == 15)
        number = jnp.where(first, jnp.where(step == 15, 7, step // 2 - 1), (step + 1) // 2)
        return jnp.where(first, 0, 1), number // 4, number % 4

    def start_y(step):
        side, h, u = item(step)
        for d in (2, 1, 3):
            y_copy(d, h, u, side).start()
        x_copy(h, u, side).start()

    def idx_copy(k, slot):
        r = (row + core) % rows
        return remote(pair_ref, idx.at[slot], idx_send.at[k], idx_recv.at[k], (r * ROW + (y + k) % ROW, seg))

    own_idx = pltpu.make_async_copy(pair_ref, idx.at[y], local.at[6])

    whiten(0)
    pl.semaphore_wait(barrier, 19 + 6 * core)
    for step in range(AHEAD):
        start_y(jnp.int32(step))
    for k in range(1, ROW):
        idx_copy(k, y).start()

    @pl.when(core == 0)
    def _():
        own_idx.start()

    @pl.when(core == 1)
    def _():
        idx_copy(0, y).start()

    give_own(0).start()
    keep_own(0).start()
    whiten(1)
    give_own(1).start()
    keep_own(1).start()
    total[...] = jnp.zeros_like(total)

    channel_row = lax.broadcasted_iota(jnp.int32, (128, 128), 0)
    source_y = (y + ROW - (channel_row // 16) % ROW) % ROW
    channel = pair_row * (ROW * CH) + source_y * CH + (channel_row // 64) * 16 + channel_row % 16

    def make_picks(slot, carry):
        at_rows = pl.ds(pl.multiple_of(slot * 128, 128), 128)

        def picks(which, shift):
            hit = channel + shift == idx[slot, which : which + 1, :]
            return jnp.where(hit, 1.0, 0.0).T.astype(jnp.bfloat16)

        first_pick[at_rows, :] = picks(0, 0)
        second_pick[at_rows, 0:128] = picks(1, 0)
        second_pick[at_rows, 128:256] = picks(1, 128)
        return carry

    def spectra(side, u, s):
        return [both[side, h, u, s].reshape(64, 256) for h in range(2)]

    def correlate(u, pairs):
        cross_re = cross_im = None
        for s in range(2 * SEG):
            near = jnp.concatenate(spectra(core, u, s), axis=0)
            far = jnp.concatenate(spectra(1 - core, u, s), axis=0)
            a = jnp.dot(first_pick[pairs], near, preferred_element_type=jnp.float32)
            b = jnp.dot(
                second_pick[pairs], jnp.concatenate([near, far], axis=0), preferred_element_type=jnp.float32
            )
            ar, ai, br, bi = a[:, :128], a[:, 128:], b[:, :128], b[:, 128:]
            re, im = ar * br + ai * bi, ai * br - ar * bi
            cross_re = re if cross_re is None else cross_re + re
            cross_im = im if cross_im is None else cross_im + im
        cross = jnp.concatenate([cross_re, cross_im], axis=1).astype(jnp.bfloat16)
        total[pairs] += jnp.dot(cross, lag[u], preferred_element_type=jnp.float32)

    def advance(step, carry):
        side, h, u = item(step)

        @pl.when(step < 16)
        def _():
            for d in (1, 3, 2):
                y_copy(d, h, u, side).wait_send()

        @pl.when(step + AHEAD < 16)
        def _():
            start_y(step + AHEAD)

        @pl.when((step < 16) & (side == core))
        def _():
            for d in (1, 3, 2):
                for c in range(2):
                    y_arrival(d, h, u, c).wait_recv()
                rest_copy(d, h, u).start()

        @pl.when(step == PICKS)
        def _():
            @pl.when(core == 0)
            def _():
                own_idx.wait()

            @pl.when(core == 1)
            def _():
                idx_copy(0, y).wait_recv()

            for k in range(1, ROW):
                idx_copy(k, (y + ROW - k) % ROW).wait_recv()
            lax.fori_loop(0, ROW, make_picks, 0)
            fetch_lag.wait()
            for h in range(2):
                keep_own(h).wait()
                take_own(h).wait_recv()

        side, h, u = item(jnp.maximum(step - DELAY, 0))

        @pl.when((side == core) & (h == 1) & (u < 3))
        def _():
            x_wait(u)
            correlate(u, pl.ds(0, 512))

        return carry

    def x_wait(u):
        for h in range(2):
            for c in range(2):
                x_arrival(h, u, c).wait_recv()
            for d in (1, 3, 2):
                rest_copy(d, h, u).wait_recv()

    lax.fori_loop(0, 15 + DELAY, advance, 0)

    def sum_copy(q, c):
        return remote(piece.at[q, c], got.at[mine], sum_send.at[q, c], sum_recv.at[mine], at(row, q, c))

    def sum_arrival(q):
        return remote(piece.at[0, 0], got.at[q], sum_send.at[0, 0], sum_recv.at[q], sibling)

    def row_copy(q):
        return remote(piece.at[q], row_got.at[mine], row_send.at[q], row_recv.at[mine], at(row, q, 1))

    def row_arrival(q):
        return remote(piece.at[q], row_got.at[q], row_send.at[q], row_recv.at[q], sibling)

    def late_copy(c):
        return remote(row_sum.at[c], late_sum, late_send.at[c], late_recv, (before * ROW + y, zh * 2 + c))

    x_wait(3)

    def finish(i, carry):
        half = (y // 2 + 1 + i) % 2
        correlate(3, pl.ds(pl.multiple_of(half * 256, 256), 256))

        for k in range(4):
            q = half * 4 + (mine + k) % 4
            for c in range(2):
                piece[q, c] = total[pl.ds(pl.multiple_of(q * 64 + c * 32, 32), 32), :].astype(jnp.bfloat16)

            @pl.when(core == 0)
            def _(q=q):
                @pl.when(q != mine)
                def _():
                    sum_copy(q, 0).start()

                sum_copy(q, 1).start()

            @pl.when((core == 1) & (q != mine))
            def _(q=q):
                row_copy(q).start()

        return carry

    lax.fori_loop(0, 2, finish, 0)

    @pl.when(core == 0)
    def _():
        got[mine] = piece[mine, 0]

    @pl.when(core == 1)
    def _():
        for k in range(1, 8):
            row_arrival((mine + k) % 8).wait_recv()
        for c in range(2):
            sums = total[pl.ds(pl.multiple_of(mine * 64 + c * 32, 32), 32), :]
            for k in range(1, 8):
                sums = sums + row_got[(mine + k) % 8, c].astype(jnp.float32)
            row_sum[c] = sums.astype(jnp.bfloat16)
            late_copy(c).start()

    def sent(u, carry):
        for h in range(2):
            for side in range(2):
                x_copy(h, u, side).wait_send()
            for d in (1, 2, 3):
                rest_copy(d, h, u).wait_send()
        return carry

    lax.fori_loop(0, 4, sent, 0)
    for h in range(2):
        give_own(h).wait_send()
    for k in range(1, ROW):
        idx_copy(k, y).wait_send()

    @pl.when(core == 1)
    def _():
        idx_copy(0, y).wait_send()
        sum_arrival(mine).wait_recv()

    widest = column(window_ref[...])
    lags = jnp.abs(lax.broadcasted_iota(jnp.int32, (32, LAGS), 1) - LAGS // 2).astype(jnp.float32)
    late_copy(0).wait_recv()
    result = late_sum[...].astype(jnp.float32)
    for k in range(1, 8):
        sum_arrival((mine + k) % 8).wait_recv()
    for k in range(8):
        result = result + got[k].astype(jnp.float32)
    out_ref[...] = jnp.where(lags <= widest, result, 0.0)
    @pl.when(core == 0)
    def _():
        for k in range(8):
            q = (mine + k) % 8
            if k:
                sum_copy(q, 0).wait_send()
            sum_copy(q, 1).wait_send()

    @pl.when(core == 1)
    def _():
        for k in range(1, 8):
            row_copy((mine + k) % 8).wait_send()
        for c in range(2):
            late_copy(c).wait_send()


def body(traces, alive, pair_chan, lag_window):
    rows = lax.axis_size("chan") // ROW
    dma = pltpu.SemaphoreType.DMA
    hbm = pl.BlockSpec(memory_space=pl.ANY)
    return pl.pallas_call(
        functools.partial(kernel, rows),
        out_shape=jax.ShapeDtypeStruct((32, LAGS), jnp.float32),
        in_specs=[hbm] * 6,
        out_specs=pl.BlockSpec(memory_space=pltpu.VMEM),
        scratch_shapes=[
            pltpu.VMEM((1, CH), jnp.int32),
            pltpu.VMEM((2, 128), jnp.int32),
            pltpu.VMEM((1, 32), jnp.int32),
            pltpu.VMEM((CH, SEG, SAMP), jnp.bfloat16),
            pltpu.VMEM((UNITS, 64, 256), jnp.float32),
            pltpu.VMEM((UNITS, 2, 64, 128), jnp.float32),
            pltpu.VMEM((64, 128), jnp.float32),
            pltpu.VMEM((UNITS, 256, 256), jnp.bfloat16),
            pltpu.VMEM((2, ROW, 8, SEG, 16, 256), jnp.bfloat16),
            pltpu.VMEM((2, 2, 4, 2 * SEG, ROW, 16, 256), jnp.bfloat16),
            pltpu.VMEM((4, 256, LAGS), jnp.bfloat16),
            pltpu.VMEM((ROW, 2, 128), jnp.int32),
            pltpu.VMEM((512, 128), jnp.bfloat16),
            pltpu.VMEM((512, 256), jnp.bfloat16),
            pltpu.VMEM((512, LAGS), jnp.float32),
            pltpu.VMEM((8, 2, 32, LAGS), jnp.bfloat16),
            pltpu.VMEM((8, 32, LAGS), jnp.bfloat16),
            pltpu.VMEM((8, 2, 32, LAGS), jnp.bfloat16),
            pltpu.VMEM((2, 32, LAGS), jnp.bfloat16),
            pltpu.VMEM((32, LAGS), jnp.bfloat16),
            dma((2, 3, 2, 4)),
            dma((2, 3, 2, 4)),
            dma((2,)),
            dma((2,)),
            dma((2, 2, 4)),
            dma((2, 2, 4)),
            dma((3, 2, 4)),
            dma((3, 2, 4)),
            dma((ROW,)),
            dma((ROW,)),
            dma((8, 2)),
            dma((8,)),
            dma((8,)),
            dma((8,)),
            dma((2,)),
            dma,
            dma((10,)),
        ],
        compiler_params=pltpu.CompilerParams(
            collective_id=0, has_side_effects=True, vmem_limit_bytes=60 * 2**20
        ),
    )(
        traces,
        alive[None],
        pair_chan.T,
        lag_window[None],
        jnp.asarray(second_table()),
        jnp.asarray(lag_table()),
    )


def solution(mesh):
    in_specs = (P("chan", "seg", None), P("chan"), P("chan", None), P(("chan", "seg")))
    out_specs = P(("chan", "seg"), None)
    return jax.shard_map(body, mesh=mesh, in_specs=in_specs, out_specs=out_specs, check_vma=False)
```

```python
import functools
import math

import jax
import jax.numpy as jnp
import numpy as np
from jax import lax
from jax.experimental import pallas as pl
from jax.experimental.pallas import tpu as pltpu
from jax.sharding import PartitionSpec as P

FREQ = 4096
SAMP = 8192
BAND = 64
LAGS = 512
UNITS = 32
ROW = 4
CH = 32
SEG = 4
EPS = 1e-06
AHEAD = 4
DELAY = 4
PICKS = 8
MESH = pl.DeviceIdType.MESH


def unit_bins():
    u = np.arange(UNITS)[:, None]
    lane = np.arange(128)[None, :]
    low = np.where(lane < 64, u, np.where(u == 0, 32, 64 - u))
    return low + 64 * (lane % 64)


def second_table():
    bins = unit_bins()[:, None, :]
    t2 = np.arange(128)[None, :, None]
    angle = 2.0 * np.pi * ((t2 * bins) % SAMP) / SAMP
    c, s = np.cos(angle), np.sin(angle)
    first = np.arange(128)[None, None, :] < 64
    unit0 = np.arange(UNITS)[:, None, None] == 0
    sign = np.where(first, 1.0, -1.0)
    rr = np.where(unit0, np.where(first, c, 0.0), c)
    ri = np.where(unit0, np.where(first, -s, 0.0), -s)
    ir = np.where(unit0, np.where(first, 0.0, c), sign * s)
    ii = np.where(unit0, np.where(first, 0.0, -s), sign * c)
    top = np.concatenate([rr, ri], axis=2)
    bottom = np.concatenate([ir, ii], axis=2)
    return np.concatenate([top, bottom], axis=1).astype(jnp.bfloat16)


def lag_table():
    bins = unit_bins()[:, :, None].astype(np.int64)
    tau = np.arange(LAGS)[None, None, :] - LAGS // 2
    angle = 2.0 * np.pi * ((bins * tau) % SAMP) / SAMP
    return (np.concatenate([np.cos(angle), -np.sin(angle)], axis=1) / 256.0).astype(jnp.bfloat16)


def real_dft(values):
    n = len(values)
    if n == 1:
        return [values[0]], [None]
    if n == 2:
        return [values[0] + values[1], values[0] - values[1]], [None, None]
    er, ei = real_dft(values[0::2])
    odr, odi = real_dft(values[1::2])
    half, quarter = n // 2, n // 4
    re, im = [None] * (half + 1), [None] * (half + 1)
    re[0], re[half] = er[0] + odr[0], er[0] - odr[0]
    re[quarter], im[quarter] = er[quarter], -odr[quarter]
    for k in range(1, quarter):
        c, s = math.cos(2 * math.pi * k / n), math.sin(2 * math.pi * k / n)
        if 8 * k == n:
            pr, pi = (odr[k] + odi[k]) * c, (odi[k] - odr[k]) * c
        else:
            pr, pi = odr[k] * c + odi[k] * s, odi[k] * c - odr[k] * s
        re[k], im[k] = er[k] + pr, ei[k] + pi
        re[half - k], im[half - k] = er[k] - pr, pi - ei[k]
    return re, im


def kernel(
    rows, traces_hbm, alive_hbm, pair_hbm, window_hbm, table_hbm, lag_hbm, out_ref,
    alive_ref, pair_ref, window_ref, x, mid, spec, level, table, w,
    both, lag, idx, first_pick, second_pick, total, piece, got, row_got, row_sum, late_sum,
    y_send, y_recv, own_send, own_recv, x_send, x_recv, rest_send, rest_recv,
    idx_send, idx_recv, sum_send, sum_recv, row_send, row_recv, late_send, late_recv, local,
):
    me, seg = lax.axis_index("chan"), lax.axis_index("seg")
    row, y = me // ROW, me % ROW
    zh, core = seg // 2, seg % 2
    before, after = (row + rows - 1) % rows, (row + 1) % rows
    mine = y * 2 + zh
    pair_row = (row + rows - core) % rows
    my_segs = pl.ds(SEG * core, SEG)

    def at(r, q, c):
        return (r * ROW + q // 2, (q % 2) * 2 + c)

    def remote(src, dst, send, recv, device):
        return pltpu.make_async_remote_copy(
            src_ref=src, dst_ref=dst, send_sem=send, recv_sem=recv, device_id=device, device_id_type=MESH
        )

    sibling = (me, zh * 2 + 1 - core)
    barrier = pltpu.get_barrier_semaphore()

    def greet(device):
        pl.semaphore_signal(barrier, inc=1, device_id=device, device_id_type=MESH)

    load = [
        pltpu.make_async_copy(traces_hbm.at[pl.ds(16 * h, 16)], x.at[pl.ds(16 * h, 16)], local.at[h]) for h in range(2)
    ]
    small = [
        pltpu.make_async_copy(src, dst, local.at[7 + k])
        for k, (src, dst) in enumerate(((alive_hbm, alive_ref), (pair_hbm, pair_ref), (window_hbm, window_ref)))
    ]
    load[0].start()
    for copy in small:
        copy.start()
    fetch_table = pltpu.make_async_copy(table_hbm, table, local.at[2])
    fetch_table.start()
    load[1].start()
    fetch_lag = pltpu.make_async_copy(lag_hbm.at[pl.ds(8 * y + 4 * core, 4)], lag, local.at[3])
    fetch_lag.start()

    greet(sibling)
    for k in range(1, 8):
        for c in range(2):
            greet(at(row, (mine + k) % 8, c))
    for r in (before, after):
        for c in range(2):
            greet((r * ROW + y, zh * 2 + c))

        @pl.when(core == 1)
        def _(r=r):
            for k in range(1, ROW):
                greet((r * ROW + (y + k) % ROW, seg))

    def column(values):
        n = values.shape[1]
        diagonal = lax.broadcasted_iota(jnp.int32, (n, n), 0) == lax.broadcasted_iota(jnp.int32, (n, n), 1)
        return jnp.sum(jnp.where(diagonal, values.astype(jnp.float32), 0.0), axis=1, keepdims=True)

    for copy in small:
        copy.wait()
    live = column(alive_ref[...])

    def whiten(h):
        load[h].wait()

        def first_stage(block, carry):
            channels = pl.ds(16 * h + 2 * block, 2)
            values = [
                x[channels, :, pl.ds(128 * t, 128)].astype(jnp.float32).reshape(8, 128) for t in range(64)
            ]
            re, im = real_dft(values)
            at_rows = pl.ds(pl.multiple_of(8 * block, 8), 8)
            mid[0, at_rows, 0:128] = re[0]
            mid[0, at_rows, 128:256] = re[32]
            for k in range(1, 32):
                mid[k, at_rows, 0:128] = re[k]
                mid[k, at_rows, 128:256] = im[k]
            return carry

        lax.fori_loop(0, 8, first_stage, 0)
        if h == 0:
            fetch_table.wait()
        level[...] = jnp.zeros_like(level)

        def second_stage(u, carry):
            result = jnp.dot(mid[u].astype(jnp.bfloat16), table[u], preferred_element_type=jnp.float32)
            re, im = result[:, :128], result[:, 128:]
            spec[u, 0] = re
            spec[u, 1] = im
            level[...] += jnp.sqrt(re * re + im * im)
            return carry

        lax.fori_loop(0, UNITS, second_stage, 0, unroll=8)
        sums = level[...]
        level[...] = 1.0 / ((sums + pltpu.roll(sums, 64, 1)) * (1.0 / BAND) + EPS)
        scales = [level[pl.ds(s, 16, stride=SEG), :] * live[16 * h : 16 * h + 16] for s in range(SEG)]

        def third_stage(u, carry):
            for s in range(SEG):
                for part in range(2):
                    value = spec[u, part, pl.ds(s, 16, stride=SEG), :] * scales[s]
                    w[h, u // 8, u % 8, s, :, pl.ds(128 * part, 128)] = value.astype(jnp.bfloat16)
            return carry

        lax.fori_loop(0, UNITS, third_stage, 0, unroll=2)

    def keep_own(h):
        return pltpu.make_async_copy(
            w.at[h, y, pl.ds(4 * core, 4)], both.at[0, h, :, my_segs, 0], local.at[4 + h]
        )

    def give_own(h):
        return remote(
            w.at[h, y, pl.ds(4 * (1 - core), 4)], both.at[0, h, :, my_segs, 0], own_send.at[h], own_recv.at[h], sibling
        )

    def take_own(h):
        other = pl.ds(SEG * (1 - core), SEG)
        return remote(w.at[h, y, pl.ds(0, 4)], both.at[0, h, :, other, 0], own_send.at[h], own_recv.at[h], sibling)

    def y_copy(d, h, u, side):
        to = (y + d) % ROW
        return remote(
            w.at[h, to, 4 * side + u], both.at[0, h, u, my_segs, d], y_send.at[side, d - 1, h, u],
            y_recv.at[core, d - 1, h, u], (row * ROW + to, zh * 2 + side),
        )

    def y_arrival(d, h, u, c):
        return remote(
            w.at[h, y, u], both.at[0, h, u, pl.ds(SEG * c, SEG), d], y_send.at[0, d - 1, h, u],
            y_recv.at[c, d - 1, h, u], sibling,
        )

    def x_copy(h, u, side):
        to = (row + rows - 1 + 2 * side) % rows
        return remote(
            w.at[h, y, 4 * side + u], both.at[1, h, u, my_segs, 0], x_send.at[side, h, u], x_recv.at[core, h, u],
            (to * ROW + y, zh * 2 + side),
        )

    def x_arrival(h, u, c):
        return remote(
            w.at[h, y, u], both.at[1, h, u, pl.ds(SEG * c, SEG), 0], x_send.at[0, h, u], x_recv.at[c, h, u], sibling
        )

    def rest_copy(d, h, u):
        to = (row + rows - 1 + 2 * core) % rows
        return remote(
            both.at[0, h, u, :, d], both.at[1, h, u, :, d], rest_send.at[d - 1, h, u], rest_recv.at[d - 1, h, u],
            (to * ROW + y, seg),
        )

    def item(step):
        first = ((step % 2 == 0) & (step >= 2)) | (step == 15)
        number = jnp.where(first, jnp.where(step == 15, 7, step // 2 - 1), (step + 1) // 2)
        return jnp.where(first, 0, 1), number // 4, number % 4

    def start_y(step):
        side, h, u = item(step)
        for d in (2, 1, 3):
            y_copy(d, h, u, side).start()
        x_copy(h, u, side).start()

    def idx_copy(k, slot):
        r = (row + core) % rows
        return remote(pair_ref, idx.at[slot], idx_send.at[k], idx_recv.at[k], (r * ROW + (y + k) % ROW, seg))

    own_idx = pltpu.make_async_copy(pair_ref, idx.at[y], local.at[6])

    whiten(0)
    pl.semaphore_wait(barrier, 19 + 6 * core)
    for step in range(AHEAD):
        start_y(jnp.int32(step))
    for k in range(1, ROW):
        idx_copy(k, y).start()

    @pl.when(core == 0)
    def _():
        own_idx.start()

    @pl.when(core == 1)
    def _():
        idx_copy(0, y).start()

    give_own(0).start()
    keep_own(0).start()
    whiten(1)
    give_own(1).start()
    keep_own(1).start()

    channel_row = lax.broadcasted_iota(jnp.int32, (128, 128), 0)
    source_y = (y + ROW - (channel_row // 16) % ROW) % ROW
    channel = pair_row * (ROW * CH) + source_y * CH + (channel_row // 64) * 16 + channel_row % 16

    def make_picks(slot, carry):
        at_rows = pl.ds(pl.multiple_of(slot * 128, 128), 128)

        def picks(which, shift):
            hit = channel + shift == idx[slot, which : which + 1, :]
            return jnp.where(hit, 1.0, 0.0).T.astype(jnp.bfloat16)

        first_pick[at_rows, :] = picks(0, 0)
        second_pick[at_rows, 0:128] = picks(1, 0)
        second_pick[at_rows, 128:256] = picks(1, 128)
        return carry

    def spectra(side, u, s):
        return [both[side, h, u, s].reshape(64, 256) for h in range(2)]

    def correlate(u, pairs):
        cross_re = cross_im = None
        for s in range(2 * SEG):
            near = jnp.concatenate(spectra(core, u, s), axis=0)
            far = jnp.concatenate(spectra(1 - core, u, s), axis=0)
            a = jnp.dot(first_pick[pairs], near, preferred_element_type=jnp.float32)
            b = jnp.dot(
                second_pick[pairs], jnp.concatenate([near, far], axis=0), preferred_element_type=jnp.float32
            )
            ar, ai, br, bi = a[:, :128], a[:, 128:], b[:, :128], b[:, 128:]
            re, im = ar * br + ai * bi, ai * br - ar * bi
            cross_re = re if cross_re is None else cross_re + re
            cross_im = im if cross_im is None else cross_im + im
        cross = jnp.concatenate([cross_re, cross_im], axis=1).astype(jnp.bfloat16)
        total[pairs] += jnp.dot(cross, lag[u], preferred_element_type=jnp.float32)

    def advance(step, carry):
        side, h, u = item(step)

        @pl.when(step < 16)
        def _():
            for d in (1, 3, 2):
                y_copy(d, h, u, side).wait_send()

        @pl.when(step + AHEAD < 16)
        def _():
            start_y(step + AHEAD)

        @pl.when((step < 16) & (side == core))
        def _():
            for d in (1, 3, 2):
                for c in range(2):
                    y_arrival(d, h, u, c).wait_recv()
                rest_copy(d, h, u).start()

        @pl.when(step == PICKS)
        def _():
            @pl.when(core == 0)
            def _():
                own_idx.wait()

            @pl.when(core == 1)
            def _():
                idx_copy(0, y).wait_recv()

            for k in range(1, ROW):
                idx_copy(k, (y + ROW - k) % ROW).wait_recv()
            lax.fori_loop(0, ROW, make_picks, 0)
            fetch_lag.wait()
            for h in range(2):
                keep_own(h).wait()
                take_own(h).wait_recv()

        side, h, u = item(jnp.maximum(step - DELAY, 0))

        @pl.when((side == core) & (h == 1) & (u < 3))
        def _():
            @pl.when(u == 0)
            def _():
                total[...] = jnp.zeros_like(total)

            x_wait(u)
            correlate(u, pl.ds(0, 512))

        return carry

    def x_wait(u):
        for h in range(2):
            for c in range(2):
                x_arrival(h, u, c).wait_recv()
            for d in (1, 3, 2):
                rest_copy(d, h, u).wait_recv()

    lax.fori_loop(0, 15 + DELAY, advance, 0)

    def sum_copy(q, c):
        return remote(piece.at[q, c], got.at[mine], sum_send.at[q, c], sum_recv.at[mine], at(row, q, c))

    def sum_arrival(q):
        return remote(piece.at[0, 0], got.at[q], sum_send.at[0, 0], sum_recv.at[q], sibling)

    def row_copy(q):
        return remote(piece.at[q], row_got.at[mine], row_send.at[q], row_recv.at[mine], at(row, q, 1))

    def row_arrival(q):
        return remote(piece.at[q], row_got.at[q], row_send.at[q], row_recv.at[q], sibling)

    def late_copy(c):
        return remote(row_sum.at[c], late_sum, late_send.at[c], late_recv, (before * ROW + y, zh * 2 + c))

    x_wait(3)

    def finish(i, carry):
        half = (y // 2 + 1 + i) % 2
        correlate(3, pl.ds(pl.multiple_of(half * 256, 256), 256))

        for k in range(4):
            q = half * 4 + (mine + k) % 4
            for c in range(2):
                piece[q, c] = total[pl.ds(pl.multiple_of(q * 64 + c * 32, 32), 32), :].astype(jnp.bfloat16)

            @pl.when(core == 0)
            def _(q=q):
                @pl.when(q != mine)
                def _():
                    sum_copy(q, 0).start()

                sum_copy(q, 1).start()

            @pl.when((core == 1) & (q != mine))
            def _(q=q):
                row_copy(q).start()

        return carry

    lax.fori_loop(0, 2, finish, 0)

    @pl.when(core == 0)
    def _():
        got[mine] = piece[mine, 0]

    @pl.when(core == 1)
    def _():
        for k in range(1, 8):
            row_arrival((mine + k) % 8).wait_recv()
        for c in range(2):
            sums = total[pl.ds(pl.multiple_of(mine * 64 + c * 32, 32), 32), :]
            for k in range(1, 8):
                sums = sums + row_got[(mine + k) % 8, c].astype(jnp.float32)
            row_sum[c] = sums.astype(jnp.bfloat16)
            late_copy(c).start()

    def sent(u, carry):
        for h in range(2):
            for side in range(2):
                x_copy(h, u, side).wait_send()
            for d in (1, 2, 3):
                rest_copy(d, h, u).wait_send()
        return carry

    lax.fori_loop(0, 4, sent, 0)
    for h in range(2):
        give_own(h).wait_send()
    for k in range(1, ROW):
        idx_copy(k, y).wait_send()

    @pl.when(core == 1)
    def _():
        idx_copy(0, y).wait_send()
        sum_arrival(mine).wait_recv()

    widest = column(window_ref[...])
    lags = jnp.abs(lax.broadcasted_iota(jnp.int32, (32, LAGS), 1) - LAGS // 2).astype(jnp.float32)
    late_copy(0).wait_recv()
    result = late_sum[...].astype(jnp.float32)
    for k in range(1, 8):
        sum_arrival((mine + k) % 8).wait_recv()
    for k in range(8):
        result = result + got[k].astype(jnp.float32)
    out_ref[...] = jnp.where(lags <= widest, result, 0.0)
    @pl.when(core == 0)
    def _():
        for k in range(8):
            q = (mine + k) % 8
            if k:
                sum_copy(q, 0).wait_send()
            sum_copy(q, 1).wait_send()

    @pl.when(core == 1)
    def _():
        for k in range(1, 8):
            row_copy((mine + k) % 8).wait_send()
        for c in range(2):
            late_copy(c).wait_send()


def body(traces, alive, pair_chan, lag_window):
    rows = lax.axis_size("chan") // ROW
    dma = pltpu.SemaphoreType.DMA
    hbm = pl.BlockSpec(memory_space=pl.ANY)
    return pl.pallas_call(
        functools.partial(kernel, rows),
        out_shape=jax.ShapeDtypeStruct((32, LAGS), jnp.float32),
        in_specs=[hbm] * 6,
        out_specs=pl.BlockSpec(memory_space=pltpu.VMEM),
        scratch_shapes=[
            pltpu.VMEM((1, CH), jnp.int32),
            pltpu.VMEM((2, 128), jnp.int32),
            pltpu.VMEM((1, 32), jnp.int32),
            pltpu.VMEM((CH, SEG, SAMP), jnp.bfloat16),
            pltpu.VMEM((UNITS, 64, 256), jnp.float32),
            pltpu.VMEM((UNITS, 2, 64, 128), jnp.float32),
            pltpu.VMEM((64, 128), jnp.float32),
            pltpu.VMEM((UNITS, 256, 256), jnp.bfloat16),
            pltpu.VMEM((2, ROW, 8, SEG, 16, 256), jnp.bfloat16),
            pltpu.VMEM((2, 2, 4, 2 * SEG, ROW, 16, 256), jnp.bfloat16),
            pltpu.VMEM((4, 256, LAGS), jnp.bfloat16),
            pltpu.VMEM((ROW, 2, 128), jnp.int32),
            pltpu.VMEM((512, 128), jnp.bfloat16),
            pltpu.VMEM((512, 256), jnp.bfloat16),
            pltpu.VMEM((512, LAGS), jnp.float32),
            pltpu.VMEM((8, 2, 32, LAGS), jnp.bfloat16),
            pltpu.VMEM((8, 32, LAGS), jnp.bfloat16),
            pltpu.VMEM((8, 2, 32, LAGS), jnp.bfloat16),
            pltpu.VMEM((2, 32, LAGS), jnp.bfloat16),
            pltpu.VMEM((32, LAGS), jnp.bfloat16),
            dma((2, 3, 2, 4)),
            dma((2, 3, 2, 4)),
            dma((2,)),
            dma((2,)),
            dma((2, 2, 4)),
            dma((2, 2, 4)),
            dma((3, 2, 4)),
            dma((3, 2, 4)),
            dma((ROW,)),
            dma((ROW,)),
            dma((8, 2)),
            dma((8,)),
            dma((8,)),
            dma((8,)),
            dma((2,)),
            dma,
            dma((10,)),
        ],
        compiler_params=pltpu.CompilerParams(
            collective_id=0, has_side_effects=True, vmem_limit_bytes=60 * 2**20
        ),
    )(
        traces,
        alive[None],
        pair_chan.T,
        lag_window[None],
        jnp.asarray(second_table()),
        jnp.asarray(lag_table()),
    )


def solution(mesh):
    in_specs = (P("chan", "seg", None), P("chan"), P("chan", None), P(("chan", "seg")))
    out_specs = P(("chan", "seg"), None)
    return jax.shard_map(body, mesh=mesh, in_specs=in_specs, out_specs=out_specs, check_vma=False)
```

```python
import functools
import math

import jax
import jax.numpy as jnp
import numpy as np
from jax import lax
from jax.experimental import pallas as pl
from jax.experimental.pallas import tpu as pltpu
from jax.sharding import PartitionSpec as P

FREQ = 4096
SAMP = 8192
BAND = 64
LAGS = 512
UNITS = 32
ROW = 4
CH = 32
SEG = 4
EPS = 1e-06
AHEAD = 4
DELAY = 4
PICKS = 8
MESH = pl.DeviceIdType.MESH


def unit_bins():
    u = np.arange(UNITS)[:, None]
    lane = np.arange(128)[None, :]
    low = np.where(lane < 64, u, np.where(u == 0, 32, 64 - u))
    return low + 64 * (lane % 64)


def second_table():
    bins = unit_bins()[:, None, :]
    t2 = np.arange(128)[None, :, None]
    angle = 2.0 * np.pi * ((t2 * bins) % SAMP) / SAMP
    c, s = np.cos(angle), np.sin(angle)
    first = np.arange(128)[None, None, :] < 64
    unit0 = np.arange(UNITS)[:, None, None] == 0
    sign = np.where(first, 1.0, -1.0)
    rr = np.where(unit0, np.where(first, c, 0.0), c)
    ri = np.where(unit0, np.where(first, -s, 0.0), -s)
    ir = np.where(unit0, np.where(first, 0.0, c), sign * s)
    ii = np.where(unit0, np.where(first, 0.0, -s), sign * c)
    top = np.concatenate([rr, ri], axis=2)
    bottom = np.concatenate([ir, ii], axis=2)
    return np.concatenate([top, bottom], axis=1).astype(jnp.bfloat16)


def lag_table():
    bins = unit_bins()[:, :, None].astype(np.int64)
    tau = np.arange(LAGS)[None, None, :] - LAGS // 2
    angle = 2.0 * np.pi * ((bins * tau) % SAMP) / SAMP
    return (np.concatenate([np.cos(angle), -np.sin(angle)], axis=1) / 256.0).astype(jnp.bfloat16)


def real_dft(values):
    n = len(values)
    if n == 1:
        return [values[0]], [None]
    if n == 2:
        return [values[0] + values[1], values[0] - values[1]], [None, None]
    er, ei = real_dft(values[0::2])
    odr, odi = real_dft(values[1::2])
    half, quarter = n // 2, n // 4
    re, im = [None] * (half + 1), [None] * (half + 1)
    re[0], re[half] = er[0] + odr[0], er[0] - odr[0]
    re[quarter], im[quarter] = er[quarter], -odr[quarter]
    for k in range(1, quarter):
        c, s = math.cos(2 * math.pi * k / n), math.sin(2 * math.pi * k / n)
        if 8 * k == n:
            pr, pi = (odr[k] + odi[k]) * c, (odi[k] - odr[k]) * c
        else:
            pr, pi = odr[k] * c + odi[k] * s, odi[k] * c - odr[k] * s
        re[k], im[k] = er[k] + pr, ei[k] + pi
        re[half - k], im[half - k] = er[k] - pr, pi - ei[k]
    return re, im


def kernel(
    rows, traces_hbm, alive_hbm, pair_hbm, window_hbm, table_hbm, lag_hbm, out_ref,
    alive_ref, pair_ref, window_ref, x, mid, spec, level, table, w,
    both, lag, idx, first_pick, second_pick, total, piece, got, row_got, row_sum, late_sum,
    y_send, y_recv, own_send, own_recv, x_send, x_recv, rest_send, rest_recv,
    idx_send, idx_recv, sum_send, sum_recv, row_send, row_recv, late_send, late_recv, local,
):
    me, seg = lax.axis_index("chan"), lax.axis_index("seg")
    row, y = me // ROW, me % ROW
    zh, core = seg // 2, seg % 2
    before, after = (row + rows - 1) % rows, (row + 1) % rows
    mine = y * 2 + zh
    pair_row = (row + rows - core) % rows
    my_segs = pl.ds(SEG * core, SEG)

    def at(r, q, c):
        return (r * ROW + q // 2, (q % 2) * 2 + c)

    def remote(src, dst, send, recv, device):
        return pltpu.make_async_remote_copy(
            src_ref=src, dst_ref=dst, send_sem=send, recv_sem=recv, device_id=device, device_id_type=MESH
        )

    sibling = (me, zh * 2 + 1 - core)
    barrier = pltpu.get_barrier_semaphore()

    def greet(device):
        pl.semaphore_signal(barrier, inc=1, device_id=device, device_id_type=MESH)

    load = [
        pltpu.make_async_copy(traces_hbm.at[pl.ds(16 * h, 16)], x.at[pl.ds(16 * h, 16)], local.at[h]) for h in range(2)
    ]
    small = [
        pltpu.make_async_copy(src, dst, local.at[7 + k])
        for k, (src, dst) in enumerate(((alive_hbm, alive_ref), (pair_hbm, pair_ref), (window_hbm, window_ref)))
    ]
    load[0].start()
    for copy in small:
        copy.start()
    fetch_table = pltpu.make_async_copy(table_hbm, table, local.at[2])
    fetch_table.start()
    load[1].start()
    fetch_lag = pltpu.make_async_copy(lag_hbm.at[pl.ds(8 * y + 4 * core, 4)], lag, local.at[3])
    fetch_lag.start()

    greet(sibling)
    for k in range(1, 8):
        for c in range(2):
            greet(at(row, (mine + k) % 8, c))
    for r in (before, after):
        for c in range(2):
            greet((r * ROW + y, zh * 2 + c))

        @pl.when(core == 1)
        def _(r=r):
            for k in range(1, ROW):
                greet((r * ROW + (y + k) % ROW, seg))

    def column(values):
        n = values.shape[1]
        diagonal = lax.broadcasted_iota(jnp.int32, (n, n), 0) == lax.broadcasted_iota(jnp.int32, (n, n), 1)
        return jnp.sum(jnp.where(diagonal, values.astype(jnp.float32), 0.0), axis=1, keepdims=True)

    for copy in small:
        copy.wait()
    live = column(alive_ref[...])

    def whiten(h):
        load[h].wait()

        def first_stage(block, carry):
            channels = pl.ds(16 * h + 2 * block, 2)
            values = [
                x[channels, :, pl.ds(128 * t, 128)].astype(jnp.float32).reshape(8, 128) for t in range(64)
            ]
            re, im = real_dft(values)
            at_rows = pl.ds(pl.multiple_of(8 * block, 8), 8)
            mid[0, at_rows, 0:128] = re[0]
            mid[0, at_rows, 128:256] = re[32]
            for k in range(1, 32):
                mid[k, at_rows, 0:128] = re[k]
                mid[k, at_rows, 128:256] = im[k]
            return carry

        lax.fori_loop(0, 8, first_stage, 0)
        if h == 0:
            fetch_table.wait()
        level[...] = jnp.zeros_like(level)

        def second_stage(u, carry):
            result = jnp.dot(mid[u].astype(jnp.bfloat16), table[u], preferred_element_type=jnp.float32)
            re, im = result[:, :128], result[:, 128:]
            spec[u, 0] = re
            spec[u, 1] = im
            level[...] += jnp.sqrt(re * re + im * im)
            return carry

        lax.fori_loop(0, UNITS, second_stage, 0, unroll=8)
        sums = level[...]
        level[...] = 1.0 / ((sums + pltpu.roll(sums, 64, 1)) * (1.0 / BAND) + EPS)
        scales = [level[pl.ds(s, 16, stride=SEG), :] * live[16 * h : 16 * h + 16] for s in range(SEG)]

        def third_stage(u, carry):
            for s in range(SEG):
                for part in range(2):
                    value = spec[u, part, pl.ds(s, 16, stride=SEG), :] * scales[s]
                    w[h, u // 8, u % 8, s, :, pl.ds(128 * part, 128)] = value.astype(jnp.bfloat16)
            return carry

        lax.fori_loop(0, UNITS, third_stage, 0, unroll=2)

    def keep_own(h):
        return pltpu.make_async_copy(
            w.at[h, y, pl.ds(4 * core, 4)], both.at[0, h, :, my_segs, 0], local.at[4 + h]
        )

    def give_own(h):
        return remote(
            w.at[h, y, pl.ds(4 * (1 - core), 4)], both.at[0, h, :, my_segs, 0], own_send.at[h], own_recv.at[h], sibling
        )

    def take_own(h):
        other = pl.ds(SEG * (1 - core), SEG)
        return remote(w.at[h, y, pl.ds(0, 4)], both.at[0, h, :, other, 0], own_send.at[h], own_recv.at[h], sibling)

    def y_copy(d, h, u, side):
        to = (y + d) % ROW
        return remote(
            w.at[h, to, 4 * side + u], both.at[0, h, u, my_segs, d], y_send.at[side, d - 1, h, u],
            y_recv.at[core, d - 1, h, u], (row * ROW + to, zh * 2 + side),
        )

    def y_arrival(d, h, u, c):
        return remote(
            w.at[h, y, u], both.at[0, h, u, pl.ds(SEG * c, SEG), d], y_send.at[0, d - 1, h, u],
            y_recv.at[c, d - 1, h, u], sibling,
        )

    def x_copy(h, u, side):
        to = (row + rows - 1 + 2 * side) % rows
        return remote(
            w.at[h, y, 4 * side + u], both.at[1, h, u, my_segs, 0], x_send.at[side, h, u], x_recv.at[core, h, u],
            (to * ROW + y, zh * 2 + side),
        )

    def x_arrival(h, u, c):
        return remote(
            w.at[h, y, u], both.at[1, h, u, pl.ds(SEG * c, SEG), 0], x_send.at[0, h, u], x_recv.at[c, h, u], sibling
        )

    def rest_copy(d, h, u):
        to = (row + rows - 1 + 2 * core) % rows
        return remote(
            both.at[0, h, u, :, d], both.at[1, h, u, :, d], rest_send.at[d - 1, h, u], rest_recv.at[d - 1, h, u],
            (to * ROW + y, seg),
        )

    def item(step):
        first = ((step % 2 == 0) & (step >= 2)) | (step == 15)
        number = jnp.where(first, jnp.where(step == 15, 7, step // 2 - 1), (step + 1) // 2)
        return jnp.where(first, 0, 1), number // 4, number % 4

    def start_y(step):
        side, h, u = item(step)
        for d in (2, 1, 3):
            y_copy(d, h, u, side).start()
        x_copy(h, u, side).start()

    def idx_copy(k, slot):
        r = (row + core) % rows
        return remote(pair_ref, idx.at[slot], idx_send.at[k], idx_recv.at[k], (r * ROW + (y + k) % ROW, seg))

    own_idx = pltpu.make_async_copy(pair_ref, idx.at[y], local.at[6])

    whiten(0)
    pl.semaphore_wait(barrier, 19 + 6 * core)
    for step in range(AHEAD):
        start_y(jnp.int32(step))
    for k in range(1, ROW):
        idx_copy(k, y).start()

    @pl.when(core == 0)
    def _():
        own_idx.start()

    @pl.when(core == 1)
    def _():
        idx_copy(0, y).start()

    give_own(0).start()
    keep_own(0).start()
    whiten(1)
    give_own(1).start()
    keep_own(1).start()
    total[...] = jnp.zeros_like(total)

    channel_row = lax.broadcasted_iota(jnp.int32, (128, 128), 0)
    source_y = (y + ROW - (channel_row // 16) % ROW) % ROW
    channel = pair_row * (ROW * CH) + source_y * CH + (channel_row // 64) * 16 + channel_row % 16

    def make_picks(slot, carry):
        at_rows = pl.ds(pl.multiple_of(slot * 128, 128), 128)

        def picks(which, shift):
            hit = channel + shift == idx[slot, which : which + 1, :]
            return jnp.where(hit, 1.0, 0.0).T.astype(jnp.bfloat16)

        first_pick[at_rows, :] = picks(0, 0)
        second_pick[at_rows, 0:128] = picks(1, 0)
        second_pick[at_rows, 128:256] = picks(1, 128)
        return carry

    def spectra(side, u, s):
        return [both[side, h, u, s].reshape(64, 256) for h in range(2)]

    def correlate(u, pairs):
        cross_re = cross_im = None
        for s in range(2 * SEG):
            near = jnp.concatenate(spectra(core, u, s), axis=0)
            far = jnp.concatenate(spectra(1 - core, u, s), axis=0)
            a = jnp.dot(first_pick[pairs], near, preferred_element_type=jnp.float32)
            b = jnp.dot(
                second_pick[pairs], jnp.concatenate([near, far], axis=0), preferred_element_type=jnp.float32
            )
            ar, ai, br, bi = a[:, :128], a[:, 128:], b[:, :128], b[:, 128:]
            re, im = ar * br + ai * bi, ai * br - ar * bi
            cross_re = re if cross_re is None else cross_re + re
            cross_im = im if cross_im is None else cross_im + im
        cross = jnp.concatenate([cross_re, cross_im], axis=1).astype(jnp.bfloat16)
        total[pairs] += jnp.dot(cross, lag[u], preferred_element_type=jnp.float32)

    def advance(step, carry):
        side, h, u = item(step)

        @pl.when(step < 16)
        def _():
            for d in (1, 3, 2):
                y_copy(d, h, u, side).wait_send()

        @pl.when(step + AHEAD < 16)
        def _():
            start_y(step + AHEAD)

        @pl.when((step < 16) & (side == core))
        def _():
            for d in (1, 3, 2):
                for c in range(2):
                    y_arrival(d, h, u, c).wait_recv()
                rest_copy(d, h, u).start()

        @pl.when(step == PICKS)
        def _():
            @pl.when(core == 0)
            def _():
                own_idx.wait()

            @pl.when(core == 1)
            def _():
                idx_copy(0, y).wait_recv()

            for k in range(1, ROW):
                idx_copy(k, (y + ROW - k) % ROW).wait_recv()
            lax.fori_loop(0, ROW, make_picks, 0)
            fetch_lag.wait()
            for h in range(2):
                keep_own(h).wait()
                take_own(h).wait_recv()

        side, h, u = item(jnp.maximum(step - DELAY, 0))

        @pl.when((side == core) & (h == 1) & (u < 3))
        def _():
            x_wait(u)
            correlate(u, pl.ds(0, 512))

        return carry

    def x_wait(u):
        for h in range(2):
            for c in range(2):
                x_arrival(h, u, c).wait_recv()
            for d in (1, 3, 2):
                rest_copy(d, h, u).wait_recv()

    lax.fori_loop(0, 15 + DELAY, advance, 0)

    def sum_copy(q, c):
        return remote(piece.at[q, c], got.at[mine], sum_send.at[q, c], sum_recv.at[mine], at(row, q, c))

    def sum_arrival(q):
        return remote(piece.at[0, 0], got.at[q], sum_send.at[0, 0], sum_recv.at[q], sibling)

    def row_copy(q):
        return remote(piece.at[q], row_got.at[mine], row_send.at[q], row_recv.at[mine], at(row, q, 1))

    def row_arrival(q):
        return remote(piece.at[q], row_got.at[q], row_send.at[q], row_recv.at[q], sibling)

    def late_copy(c):
        return remote(row_sum.at[c], late_sum, late_send.at[c], late_recv, (before * ROW + y, zh * 2 + c))

    x_wait(3)

    def finish(i, carry):
        half = (y // 2 + 1 + i) % 2
        correlate(3, pl.ds(pl.multiple_of(half * 256, 256), 256))

        for k in range(4):
            q = half * 4 + (mine + k) % 4
            for c in range(2):
                piece[q, c] = total[pl.ds(pl.multiple_of(q * 64 + c * 32, 32), 32), :].astype(jnp.bfloat16)

            @pl.when(core == 0)
            def _(q=q):
                @pl.when(q != mine)
                def _():
                    sum_copy(q, 0).start()

                sum_copy(q, 1).start()

            @pl.when((core == 1) & (q != mine))
            def _(q=q):
                row_copy(q).start()

        return carry

    lax.fori_loop(0, 2, finish, 0)

    @pl.when(core == 0)
    def _():
        got[mine] = piece[mine, 0]

    @pl.when(core == 1)
    def _():
        for k in range(1, 8):
            row_arrival((mine + k) % 8).wait_recv()
        for c in range(2):
            sums = total[pl.ds(pl.multiple_of(mine * 64 + c * 32, 32), 32), :]
            for k in range(1, 8):
                sums = sums + row_got[(mine + k) % 8, c].astype(jnp.float32)
            row_sum[c] = sums.astype(jnp.bfloat16)
            late_copy(c).start()

    def sent(u, carry):
        for h in range(2):
            for side in range(2):
                x_copy(h, u, side).wait_send()
            for d in (1, 2, 3):
                rest_copy(d, h, u).wait_send()
        return carry

    lax.fori_loop(0, 4, sent, 0)
    for h in range(2):
        give_own(h).wait_send()
    for k in range(1, ROW):
        idx_copy(k, y).wait_send()

    @pl.when(core == 1)
    def _():
        idx_copy(0, y).wait_send()
        sum_arrival(mine).wait_recv()

    widest = column(window_ref[...])
    lags = jnp.abs(lax.broadcasted_iota(jnp.int32, (32, LAGS), 1) - LAGS // 2).astype(jnp.float32)
    result = got[mine].astype(jnp.float32)
    for k in range(1, 8):
        q = (mine + k) % 8
        sum_arrival(q).wait_recv()
        result = result + got[q].astype(jnp.float32)
    late_copy(0).wait_recv()
    result = result + late_sum[...].astype(jnp.float32)
    out_ref[...] = jnp.where(lags <= widest, result, 0.0)
    @pl.when(core == 0)
    def _():
        for k in range(8):
            q = (mine + k) % 8
            if k:
                sum_copy(q, 0).wait_send()
            sum_copy(q, 1).wait_send()

    @pl.when(core == 1)
    def _():
        for k in range(1, 8):
            row_copy((mine + k) % 8).wait_send()
        for c in range(2):
            late_copy(c).wait_send()


def body(traces, alive, pair_chan, lag_window):
    rows = lax.axis_size("chan") // ROW
    dma = pltpu.SemaphoreType.DMA
    hbm = pl.BlockSpec(memory_space=pl.ANY)
    return pl.pallas_call(
        functools.partial(kernel, rows),
        out_shape=jax.ShapeDtypeStruct((32, LAGS), jnp.float32),
        in_specs=[hbm] * 6,
        out_specs=pl.BlockSpec(memory_space=pltpu.VMEM),
        scratch_shapes=[
            pltpu.VMEM((1, CH), jnp.int32),
            pltpu.VMEM((2, 128), jnp.int32),
            pltpu.VMEM((1, 32), jnp.int32),
            pltpu.VMEM((CH, SEG, SAMP), jnp.bfloat16),
            pltpu.VMEM((UNITS, 64, 256), jnp.float32),
            pltpu.VMEM((UNITS, 2, 64, 128), jnp.float32),
            pltpu.VMEM((64, 128), jnp.float32),
            pltpu.VMEM((UNITS, 256, 256), jnp.bfloat16),
            pltpu.VMEM((2, ROW, 8, SEG, 16, 256), jnp.bfloat16),
            pltpu.VMEM((2, 2, 4, 2 * SEG, ROW, 16, 256), jnp.bfloat16),
            pltpu.VMEM((4, 256, LAGS), jnp.bfloat16),
            pltpu.VMEM((ROW, 2, 128), jnp.int32),
            pltpu.VMEM((512, 128), jnp.bfloat16),
            pltpu.VMEM((512, 256), jnp.bfloat16),
            pltpu.VMEM((512, LAGS), jnp.float32),
            pltpu.VMEM((8, 2, 32, LAGS), jnp.bfloat16),
            pltpu.VMEM((8, 32, LAGS), jnp.bfloat16),
            pltpu.VMEM((8, 2, 32, LAGS), jnp.bfloat16),
            pltpu.VMEM((2, 32, LAGS), jnp.bfloat16),
            pltpu.VMEM((32, LAGS), jnp.bfloat16),
            dma((2, 3, 2, 4)),
            dma((2, 3, 2, 4)),
            dma((2,)),
            dma((2,)),
            dma((2, 2, 4)),
            dma((2, 2, 4)),
            dma((3, 2, 4)),
            dma((3, 2, 4)),
            dma((ROW,)),
            dma((ROW,)),
            dma((8, 2)),
            dma((8,)),
            dma((8,)),
            dma((8,)),
            dma((2,)),
            dma,
            dma((10,)),
        ],
        compiler_params=pltpu.CompilerParams(
            collective_id=0, has_side_effects=True, vmem_limit_bytes=60 * 2**20
        ),
    )(
        traces,
        alive[None],
        pair_chan.T,
        lag_window[None],
        jnp.asarray(second_table()),
        jnp.asarray(lag_table()),
    )


def solution(mesh):
    in_specs = (P("chan", "seg", None), P("chan"), P("chan", None), P(("chan", "seg")))
    out_specs = P(("chan", "seg"), None)
    return jax.shard_map(body, mesh=mesh, in_specs=in_specs, out_specs=out_specs, check_vma=False)
```
